32 devices in a mesh: dp: 4 (over z), group: 4 (over x, core), tensor: 2 (over y).
Axes of the slice: x: 2, y: 2, z: 4, core: 2. Of those that a mesh axis runs over, the one named last changes fastest.
Arguments:
- attn_heads: bfloat16 [256, 8192], P('dp', ('group', 'tensor')), parts along dimension 0, may hold values from -6 to 6
- out_proj: bfloat16 [8192, 3584], P(('group', 'tensor')), may hold values from -0.0625 to 0.0625
- residual_in: bfloat16 [256, 3584], P(('dp', 'group', 'tensor')), parts along dimension 0, may hold values from -6 to 6
- norm_gain: float32 [3584], replicated, may hold values from 0.1 to 1.9
- expert_ids: int32 [256, 4], P(('dp', 'group', 'tensor')), parts along dimension 0, may hold values from 0 to 7, as said below
- gate_weights: bfloat16 [256, 4], P(('dp', 'group', 'tensor')), parts along dimension 0, may hold values from 0.19921875 to 1.5
- w_gate: bfloat16 [8, 3584, 1024], P('group', None, 'tensor'), may hold values from -0.09375 to 0.09375
- w_up: bfloat16 [8, 3584, 1024], P('group', None, 'tensor'), may hold values from -0.09375 to 0.09375
- w_down: bfloat16 [8, 1024, 3584], P('group', 'tensor'), may hold values from -0.1875 to 0.1875
Outputs:
- layer_out: bfloat16 [256, 3584], P(('dp', 'group', 'tensor')), parts along dimension 0
The draws below stay inside these ranges and needn't reach their ends.
There are 4 independent parts, one for each index of `dp`. The reference program is written for one: setup_inputs(seed, part) draws one part's arguments, and reference() takes and returns one part's arrays. A program takes and returns all parts, laid end to end along the dimension named above; an argument that names none is the same for every part. Nothing has to cross between parts.
Inputs may be any that keep to these rules, and one draw needn't show every extreme that they name: `expert_ids`: each row names 4 different experts, of at most 3 node groups (expert e belongs to node group e // 2). In each aligned block of 8 rows (the rows of one device) at most 6 rows name experts of any one node group, and in every draw some node group is named by exactly 6 rows of every block.
All inputs are finite; a program needn't handle non-finite values.
Results may differ from the reference program's by a relative error of at most 0.02.
Values may be sent and summed in bfloat16 or wider, within the bound.
A program may use at most 64 MiB of HBM per device.

```python
import jax
import jax.numpy as jnp
from jax import lax

D = 3584
FFE = 1024
EXP_NODE = 2
TOPK = 4
TOK_DEV = 8
HDH = 8192
TOKENS = 64
EXPERTS = 8
N_GROUP = 4
N_TENSOR = 2


def draw_expert_ids(key, part):
    blocks = TOKENS // TOK_DEV
    subkeys = jax.random.split(jax.random.fold_in(key, 11), 7)
    groups = jnp.arange(4, dtype=jnp.int32)
    rank_scores = jax.random.randint(subkeys[0], (blocks, TOK_DEV), 0, 1 << 20) * TOK_DEV + jnp.arange(TOK_DEV, dtype=jnp.int32)[None, :]
    permuted = jnp.argsort(rank_scores, axis=1).astype(jnp.int32)
    excluded = permuted % 4
    full_group = jax.random.randint(subkeys[1], (1, 1, 1), 0, 4)
    candidate = (groups[None, None, :] != excluded[:, :, None]) & (groups[None, None, :] != full_group)
    scores = jax.random.randint(subkeys[2], (blocks, TOK_DEV, 4), 1, 1 << 20) * 4 + groups[None, None, :]
    second = jnp.argmax(jnp.where(candidate, scores, -1), axis=2).astype(jnp.int32)
    dropping = jax.random.randint(subkeys[3], (blocks, TOK_DEV, 1), 0, 2)
    group_used = (groups[None, None, :] != excluded[:, :, None]) & jnp.logical_not((dropping == 1) & (groups[None, None, :] == second[:, :, None]))
    double_scores = jax.random.randint(subkeys[4], (blocks, TOK_DEV, 4), 1, 1 << 20) * 4 + groups[None, None, :]
    doubled = jnp.argmax(jnp.where(group_used, double_scores, -1), axis=2).astype(jnp.int32)
    used_count = jnp.sum(group_used.astype(jnp.int32), axis=2, keepdims=True)
    takes_both = group_used & ((used_count == 2) | (groups[None, None, :] == doubled[:, :, None]))
    expert_bit = jax.random.randint(subkeys[5], (blocks, TOK_DEV, 4), 0, 2)
    take_first = takes_both | group_used & (expert_bit == 0)
    take_second = takes_both | group_used & (expert_bit == 1)
    expert_flags = jnp.stack([take_first, take_second], axis=3).reshape(blocks, TOK_DEV, 8)
    sort_keys = jnp.where(expert_flags, 0, 8) + jnp.arange(8, dtype=jnp.int32)[None, None, :]
    chosen = jnp.argsort(sort_keys, axis=2)[:, :, :TOPK].astype(jnp.int32)
    mix_scores = jax.random.randint(subkeys[6], (blocks, TOK_DEV, TOPK), 0, 1 << 20) * TOPK + jnp.arange(TOPK, dtype=jnp.int32)[None, None, :]
    mixing = jnp.argsort(mix_scores, axis=2)
    chosen = jnp.take_along_axis(chosen, mixing, axis=2)
    return chosen.reshape(TOKENS, TOPK).astype(jnp.int32)


def steps_of(stream_key, shape, shards, smallest, top_value):
    factor_of = 1.0
    for dim, blocks in shards:
        heights = jax.random.uniform(jax.random.fold_in(jax.random.fold_in(stream_key, 6), dim), (blocks,), jnp.float32, smallest / len(shards), top_value / len(shards))
        factor_of = factor_of * jnp.repeat(jnp.exp(heights), shape[dim] // blocks).reshape((-1,) + (1,) * (len(shape) - 1 - dim))
    return factor_of


def noise(rng, shape, scale, most, cuts=(), held_as=jnp.bfloat16):
    factor_of = steps_of(rng, shape, cuts, -0.22, 0.18) if cuts else 1.0
    drawn = jax.random.normal(rng, shape, jnp.float32) * scale * factor_of
    return jnp.minimum(jnp.maximum(drawn, -most), most).astype(held_as)


def setup_inputs(seed: int = 0, part: int = 0) -> dict:
    splits = jax.random.split(jax.random.key(seed), 10)
    part_keys = jax.random.split(jax.random.fold_in(splits[9], part), 10)
    return {
        "attn_heads": noise(part_keys[0], (TOKENS, HDH), 1.0, 6.0, ((1, 8),)),
        "out_proj": noise(splits[1], (HDH, D), HDH ** -0.5, 0.0625, ((0, 8),)),
        "residual_in": noise(part_keys[2], (TOKENS, D), 1.0, 6.0, ((0, 8),)),
        "norm_gain": jnp.clip(1.0 + 0.18 * jax.random.normal(splits[3], (D,), jnp.float32), 0.1, 1.9),
        "expert_ids": draw_expert_ids(jax.random.fold_in(jax.random.fold_in(splits[9], part), 71), part),
        "gate_weights": jnp.clip(0.19921875 + 1.3007812 * jax.random.uniform(part_keys[5], (TOKENS, TOPK), jnp.float32) ** steps_of(part_keys[5], (TOKENS, TOPK), ((0, 8),), -0.2, 0.2), 0.19921875, 1.5).astype(jnp.bfloat16),
        "w_gate": noise(splits[6], (EXPERTS, D, FFE), D ** -0.5, 0.09375, ((0, 4), (2, 2))),
        "w_up": noise(splits[7], (EXPERTS, D, FFE), D ** -0.5, 0.09375, ((0, 4), (2, 2))),
        "w_down": noise(splits[8], (EXPERTS, FFE, D), FFE ** -0.5, 0.1875, ((0, 4), (1, 2))),
    }


def reference(attn_heads, out_proj, residual_in, norm_gain, expert_ids, gate_weights, w_gate, w_up, w_down):
    projected = jnp.dot(attn_heads, out_proj, preferred_element_type=jnp.float32).astype(jnp.bfloat16)
    hidden = (residual_in.astype(jnp.float32) + projected.astype(jnp.float32)).astype(jnp.bfloat16)
    stream = hidden.astype(jnp.float32)
    scale = lax.rsqrt(lax.optimization_barrier(jnp.mean(stream * stream, axis=1, keepdims=True)) + 1e-06)
    normed = (stream * scale * norm_gain).astype(jnp.bfloat16)
    matches = (expert_ids[:, :, None] == jnp.arange(EXPERTS, dtype=jnp.int32)[None, None, :]).astype(jnp.float32)
    routing = lax.optimization_barrier(jnp.sum(matches * gate_weights.astype(jnp.float32)[:, :, None], axis=1))
    block_width = FFE // N_TENSOR
    mixture = jnp.zeros((TOKENS, D), jnp.float32)
    for node_index in range(N_GROUP):
        activations = []
        for member in range(EXP_NODE):
            expert = node_index * EXP_NODE + member
            gate_proj = jnp.dot(normed, w_gate[expert], preferred_element_type=jnp.float32)
            up_proj = jnp.dot(normed, w_up[expert], preferred_element_type=jnp.float32)
            activations.append((jax.nn.silu(gate_proj) * up_proj).astype(jnp.bfloat16))
        node_sum = jnp.zeros((TOKENS, D), jnp.float32)
        for block_index in range(N_TENSOR):
            low = block_index * block_width
            block_sum = jnp.zeros((TOKENS, D), jnp.float32)
            for member in range(EXP_NODE):
                expert = node_index * EXP_NODE + member
                block_sum = block_sum + routing[:, expert:expert + 1] * jnp.dot(activations[member][:, low:low + block_width], w_down[expert, low:low + block_width, :], preferred_element_type=jnp.float32)
            rounded = lax.optimization_barrier(block_sum.astype(jnp.bfloat16))
            node_sum = node_sum + rounded.astype(jnp.float32)
        node_rounded = lax.optimization_barrier(node_sum.astype(jnp.bfloat16))
        mixture = mixture + node_rounded.astype(jnp.float32)
    return (stream + mixture).astype(jnp.bfloat16)
```

```python
import functools

import jax
import jax.numpy as jnp
from jax import lax
from jax.experimental import pallas as pl
from jax.experimental.pallas import tpu as pltpu
from jax.sharding import PartitionSpec as P

MESH = pl.DeviceIdType.MESH
F32 = jnp.float32
BF16 = jnp.bfloat16
META = 128
LAG = 3


def column_chunks(features, most=7):
    for width in (256, 128):
        if features % width == 0:
            tiles = features // width
            return max(n for n in range(1, min(most, tiles) + 1) if tiles % n == 0)
    return 1


def kernel(
    dims,
    attn_hbm, wo_hbm, res_hbm, gain_hbm, ids_hbm, gw_hbm, wg_hbm, wu_hbm, wd_hbm,
    out_hbm,
    attn_v, attn_blocks, attn_p, res_v, gain_v, ids_v, gw_v,
    wo_v, wg_v, wu_v, wd_v,
    keep1, send1, recv1, own2, send2, recv2, hidden_v, square_v,
    rows_own, rows_sib, meta_own, meta_sib,
    acc_gate, acc_up, act_v,
    keep4, send4, recv4, own5, send5, recv5, out_v,
    small_sem, wo_sem, wg_sem, wu_sem, wd_sem, out_sem,
    stage_send, stage_recv,
):
    chunks, width, chips, tensors, rows, members, experts_all = dims
    half = chips * rows
    group, tensor = lax.axis_index("group"), lax.axis_index("tensor")
    high, low = lax.div(group, 2), lax.rem(group, 2)
    place = high * tensors + tensor

    def device(position, side):
        position = lax.rem(position + chips, chips)
        return {"group": lax.div(position, tensors) * 2 + side, "tensor": lax.rem(position, tensors)}

    sibling = {"group": high * 2 + 1 - low, "tensor": tensor}

    barrier = pltpu.get_barrier_semaphore()
    pl.semaphore_signal(barrier, inc=1, device_id=sibling, device_id_type=MESH)
    for offset in range(1, chips):
        pl.semaphore_signal(
            barrier, inc=1, device_id=device(place + offset, low), device_id_type=MESH
        )

    def cols(c):
        return pl.ds(c * width, width)

    smalls = [
        pltpu.make_async_copy(src, dst, small_sem.at[i])
        for i, (src, dst) in enumerate(
            [(attn_hbm, attn_v), (res_hbm, res_v), (gain_hbm, gain_v), (ids_hbm, ids_v), (gw_hbm, gw_v)]
        )
    ]
    wo_copies = [
        pltpu.make_async_copy(wo_hbm.at[:, cols(c)], wo_v.at[c], wo_sem.at[c]) for c in range(chunks)
    ]
    wg_copies = [
        pltpu.make_async_copy(wg_hbm.at[:, cols(c), :], wg_v.at[c], wg_sem.at[c])
        for c in range(chunks)
    ]
    wu_copies = [
        pltpu.make_async_copy(wu_hbm.at[:, cols(c), :], wu_v.at[c], wu_sem.at[c])
        for c in range(chunks)
    ]
    wd_copies = [
        pltpu.make_async_copy(wd_hbm.at[:, :, cols(c)], wd_v.at[c], wd_sem.at[c])
        for c in range(chunks)
    ]
    smalls[0].start()
    wo_copies[0].start()
    for copy in smalls[1:]:
        copy.start()
    for copy in wo_copies[1:]:
        copy.start()
    for c in range(chunks):
        wg_copies[c].start()
        wu_copies[c].start()
    for copy in wd_copies:
        copy.start()

    def wait_bytes(ref, sem):
        pltpu.make_async_copy(ref, ref, sem).wait()

    def to_sibling(stage, c, src, dst):
        pltpu.make_async_remote_copy(
            src_ref=src, dst_ref=dst, send_sem=stage_send.at[stage, c],
            recv_sem=stage_recv.at[stage, c], device_id=sibling, device_id_type=MESH,
        ).start()

    def to_owners(stage, c, src, dst):
        for offset in range(1, chips):
            pltpu.make_async_remote_copy(
                src_ref=src.at[offset - 1], dst_ref=dst.at[offset - 1],
                send_sem=stage_send.at[stage, c], recv_sem=stage_recv.at[stage, c],
                device_id=device(place - offset, low), device_id_type=MESH,
            ).start()

    def to_chips(stage, c, block):
        for offset in range(1, chips):
            pltpu.make_async_remote_copy(
                src_ref=block.at[0], dst_ref=block.at[offset],
                send_sem=stage_send.at[stage, c], recv_sem=stage_recv.at[stage, c],
                device_id=device(place + offset, low), device_id_type=MESH,
            ).start()

    def peers(block):
        return block.at[pl.ds(1, chips - 1)]

    smalls[0].wait()
    attn_blocks[...] = attn_v[...].astype(F32).reshape(attn_blocks.shape)
    picked = []
    for side in (low, 1 - low):
        for offset in range(chips):
            position = lax.rem(place - offset + chips, chips)
            owner = (lax.div(position, tensors) * 2 + side) * tensors + lax.rem(position, tensors)
            picked.append(attn_blocks[owner])
    attn_p[...] = jnp.concatenate(picked, axis=0).astype(BF16)

    def split(product, keep, send):
        keep[...] = product[:half].reshape(chips, rows, width)
        send[...] = product[half:].reshape(chips, rows, width).astype(BF16)

    def project(c):
        wo_copies[c].wait()
        product = jnp.dot(attn_p[...], wo_v[c], preferred_element_type=F32)
        split(product, keep1.at[c], send1.at[c])
        if c == 0:
            pl.semaphore_wait(barrier, chips)
        to_sibling(0, c, send1.at[c], recv1.at[c])

    def add_sibling(c):
        wait_bytes(recv1.at[c], stage_recv.at[0, c])
        total = keep1[c] + recv1[c].astype(F32)
        own2[c] = total[0]
        send2[c] = total[1:].astype(BF16)
        to_owners(1, c, send2.at[c], recv2.at[c])

    def finish_hidden(c):
        wait_bytes(recv2.at[c], stage_recv.at[1, c])
        if c == 0:
            for copy in smalls[1:]:
                copy.wait()
        total = own2[c] + jnp.sum(recv2[c].astype(F32), axis=0)
        here = slice(c * width, (c + 1) * width)
        projected = total.astype(BF16).astype(F32)
        hidden = (res_v[:, here].astype(F32) + projected).astype(BF16).astype(F32)
        hidden_v[c] = hidden
        square_v[...] = hidden * hidden if c == 0 else square_v[...] + hidden * hidden
        rows_own[c, 0] = (hidden * gain_v[:, here]).astype(BF16)
        to_chips(2, c, rows_own.at[c])
        if c == chunks - 1:
            send_meta()

    def send_meta():
        mean = jnp.sum(square_v[...], axis=1, keepdims=True) / (chunks * width)
        scale = lax.rsqrt(mean + 1e-06)
        lane = lax.broadcasted_iota(jnp.int32, (rows, META), 1)
        ids = ids_v[...]
        weights = gw_v[...].astype(F32)
        block = jnp.where(lane == experts_all, scale, 0.0)
        for k in range(ids.shape[1]):
            block = block + jnp.where(lane == ids[:, k : k + 1], weights[:, k : k + 1], 0.0)
        meta_own[0] = block
        to_chips(2, chunks, meta_own)

    def forward(c):
        wait_bytes(peers(rows_own.at[c]), stage_recv.at[2, c])
        to_sibling(3, c, rows_own.at[c], rows_sib.at[c])
        if c == chunks - 1:
            wait_bytes(peers(meta_own), stage_recv.at[2, chunks])
            to_sibling(3, chunks, meta_own, meta_sib)

    def experts(c):
        wg_copies[c].wait()
        wu_copies[c].wait()
        wait_bytes(rows_sib.at[c], stage_recv.at[3, c])
        both = jnp.concatenate(
            [rows_own[c].astype(F32).reshape(half, width), rows_sib[c].astype(F32).reshape(half, width)],
            axis=0,
        ).astype(BF16)
        for member in range(members):
            gate = jnp.dot(both, wg_v[c, member], preferred_element_type=F32)
            up = jnp.dot(both, wu_v[c, member], preferred_element_type=F32)
            acc_gate[member] = gate if c == 0 else acc_gate[member] + gate
            acc_up[member] = up if c == 0 else acc_up[member] + up

    def activate():
        wait_bytes(meta_sib, stage_recv.at[3, chunks])
        block = jnp.concatenate([meta_own[...].reshape(half, META), meta_sib[...].reshape(half, META)], axis=0)
        lane = lax.broadcasted_iota(jnp.int32, block.shape, 1)
        scale = block[:, experts_all : experts_all + 1]
        for member in range(members):
            weight = jnp.sum(
                jnp.where(lane == group * members + member, block, 0.0), axis=1, keepdims=True
            )
            gate = acc_gate[member] * scale
            up = acc_up[member] * scale
            act_v[member] = (gate / (1.0 + jnp.exp(-gate)) * up * weight).astype(BF16)

    def down(c):
        wd_copies[c].wait()
        product = jnp.dot(act_v[0], wd_v[c, 0], preferred_element_type=F32)
        for member in range(1, members):
            product = product + jnp.dot(act_v[member], wd_v[c, member], preferred_element_type=F32)
        split(product, keep4.at[c], send4.at[c])
        to_sibling(4, c, send4.at[c], recv4.at[c])

    def add_sibling_down(c):
        wait_bytes(recv4.at[c], stage_recv.at[4, c])
        total = keep4[c] + recv4[c].astype(F32)
        own5[c] = total[0]
        send5[c] = total[1:].astype(BF16)
        to_owners(5, c, send5.at[c], recv5.at[c])

    def finish(c):
        wait_bytes(recv5.at[c], stage_recv.at[5, c])
        total = own5[c] + jnp.sum(recv5[c].astype(F32), axis=0)
        out_v[c] = (hidden_v[c] + total).astype(BF16)
        pltpu.make_async_copy(out_v.at[c], out_hbm.at[:, cols(c)], out_sem.at[c]).start()

    def pipeline(stages):
        steps = [(c + LAG * s, -s, c, stage) for s, stage in enumerate(stages) for c in range(chunks)]
        for _, _, c, stage in sorted(steps, key=lambda step: step[:3]):
            stage(c)

    pipeline([project, add_sibling, finish_hidden, forward, experts])
    activate()
    pipeline([down, add_sibling_down, finish])

    for c in range(chunks):
        pltpu.make_async_copy(out_v.at[c], out_hbm.at[:, cols(c)], out_sem.at[c]).wait()
        wait_bytes(send1.at[c], stage_send.at[0, c])
        wait_bytes(send2.at[c], stage_send.at[1, c])
        wait_bytes(peers(rows_own.at[c]), stage_send.at[2, c])
        wait_bytes(rows_own.at[c], stage_send.at[3, c])
        wait_bytes(send4.at[c], stage_send.at[4, c])
        wait_bytes(send5.at[c], stage_send.at[5, c])
    wait_bytes(peers(meta_own), stage_send.at[2, chunks])
    wait_bytes(meta_own, stage_send.at[3, chunks])


def on_device(
    attn_heads, out_proj, residual_in, norm_gain, expert_ids, gate_weights, w_gate, w_up, w_down
):
    rows, features = residual_in.shape
    tokens, heads = attn_heads.shape
    groups = lax.axis_size("group")
    tensors = lax.axis_size("tensor")
    members, _, units = w_gate.shape
    chips = groups // 2 * tensors
    experts_all = groups * members
    chunks = column_chunks(features)
    width = features // chunks
    dims = (chunks, width, chips, tensors, rows, members, experts_all)

    def vmem(shape, dtype):
        return pltpu.VMEM(shape, dtype)

    exchange = [
        vmem((chunks, chips, rows, width), F32),
        vmem((chunks, chips, rows, width), BF16),
        vmem((chunks, chips, rows, width), BF16),
        vmem((chunks, rows, width), F32),
        vmem((chunks, chips - 1, rows, width), BF16),
        vmem((chunks, chips - 1, rows, width), BF16),
    ]
    scratch = [
        vmem((tokens, heads), BF16),
        vmem((tokens // rows, rows, heads), F32),
        vmem((tokens, heads), BF16),
        vmem((rows, features), BF16),
        vmem((1, features), F32),
        vmem(expert_ids.shape, expert_ids.dtype),
        vmem(gate_weights.shape, gate_weights.dtype),
        vmem((chunks, heads, width), BF16),
        vmem((chunks, members, width, units), BF16),
        vmem((chunks, members, width, units), BF16),
        vmem((chunks, members, units, width), BF16),
        *exchange,
        vmem((chunks, rows, width), F32),
        vmem((rows, width), F32),
        vmem((chunks, chips, rows, width), BF16),
        vmem((chunks, chips, rows, width), BF16),
        vmem((chips, rows, META), F32),
        vmem((chips, rows, META), F32),
        vmem((members, tokens, units), F32),
        vmem((members, tokens, units), F32),
        vmem((members, tokens, units), BF16),
        *exchange,
        vmem((chunks, rows, width), BF16),
        pltpu.SemaphoreType.DMA((5,)),
        pltpu.SemaphoreType.DMA((chunks,)),
        pltpu.SemaphoreType.DMA((chunks,)),
        pltpu.SemaphoreType.DMA((chunks,)),
        pltpu.SemaphoreType.DMA((chunks,)),
        pltpu.SemaphoreType.DMA((chunks,)),
        pltpu.SemaphoreType.DMA((6, chunks + 1)),
        pltpu.SemaphoreType.DMA((6, chunks + 1)),
    ]
    weights = out_proj.size + w_gate.size + w_up.size + w_down.size
    return pl.pallas_call(
        functools.partial(kernel, dims),
        out_shape=jax.ShapeDtypeStruct((rows, features), BF16),
        in_specs=[pl.BlockSpec(memory_space=pl.ANY)] * 9,
        out_specs=pl.BlockSpec(memory_space=pl.ANY),
        scratch_shapes=scratch,
        cost_estimate=pl.CostEstimate(
            flops=2 * tokens * weights, bytes_accessed=2 * weights, transcendentals=0
        ),
        compiler_params=pltpu.CompilerParams(
            collective_id=0, has_side_effects=True, vmem_limit_bytes=56 * 1024 * 1024
        ),
        name="projected_experts",
    )(
        attn_heads, out_proj, residual_in, norm_gain.reshape(1, features),
        expert_ids, gate_weights, w_gate, w_up, w_down,
    )


def solution(mesh):
    placed = (
        P("dp", ("group", "tensor")),
        P(("group", "tensor"), None),
        P(("dp", "group", "tensor"), None),
        P(),
        P(("dp", "group", "tensor"), None),
        P(("dp", "group", "tensor"), None),
        P("group", None, "tensor"),
        P("group", None, "tensor"),
        P("group", "tensor", None),
    )
    return jax.shard_map(
        on_device,
        mesh=mesh,
        in_specs=placed,
        out_specs=P(("dp", "group", "tensor"), None),
        check_vma=False,
    )
```

```python
import functools

import jax
import jax.numpy as jnp
from jax import lax
from jax.experimental import pallas as pl
from jax.experimental.pallas import tpu as pltpu
from jax.sharding import PartitionSpec as P

MESH = pl.DeviceIdType.MESH
F32 = jnp.float32
BF16 = jnp.bfloat16
META = 128
LAGS = (0, 4, 10, 17, 21)


def column_chunks(features, most=7):
    for width in (256, 128):
        if features % width == 0:
            tiles = features // width
            return max(n for n in range(1, min(most, tiles) + 1) if tiles % n == 0)
    return 1


def kernel(
    dims,
    attn_hbm, wo_hbm, res_hbm, gain_hbm, ids_hbm, gw_hbm, wg_hbm, wu_hbm, wd_hbm,
    out_hbm,
    attn_v, attn_blocks, attn_p, res_v, gain_v, ids_v, gw_v,
    wo_v, wg_v, wu_v, wd_v,
    keep1, send1, recv1, own2, send2, recv2, hidden_v, square_v, table_v,
    rows_own, rows_sib, meta_own, meta_sib,
    acc_gate, acc_up, act_v,
    keep4, send4, recv4, own5, send5, recv5, out_v,
    small_sem, wo_sem, wg_sem, wu_sem, wd_sem, out_sem,
    stage_send, stage_recv,
):
    chunks, width, chips, tensors, rows, members, experts_all = dims
    half = chips * rows
    group, tensor = lax.axis_index("group"), lax.axis_index("tensor")
    high, low = lax.div(group, 2), lax.rem(group, 2)
    place = high * tensors + tensor

    def device(position, side):
        position = lax.rem(position + chips, chips)
        return {"group": lax.div(position, tensors) * 2 + side, "tensor": lax.rem(position, tensors)}

    sibling = {"group": high * 2 + 1 - low, "tensor": tensor}

    barrier = pltpu.get_barrier_semaphore()
    pl.semaphore_signal(barrier, inc=1, device_id=sibling, device_id_type=MESH)
    for offset in range(1, chips):
        pl.semaphore_signal(
            barrier, inc=1, device_id=device(place + offset, low), device_id_type=MESH
        )

    def cols(c):
        return pl.ds(c * width, width)

    smalls = [
        pltpu.make_async_copy(src, dst, small_sem.at[i])
        for i, (src, dst) in enumerate(
            [(attn_hbm, attn_v), (res_hbm, res_v), (gain_hbm, gain_v), (ids_hbm, ids_v), (gw_hbm, gw_v)]
        )
    ]
    wo_copies = [
        pltpu.make_async_copy(wo_hbm.at[:, cols(c)], wo_v.at[c], wo_sem.at[c]) for c in range(chunks)
    ]
    wg_copies = [
        pltpu.make_async_copy(wg_hbm.at[:, cols(c), :], wg_v.at[c], wg_sem.at[c])
        for c in range(chunks)
    ]
    wu_copies = [
        pltpu.make_async_copy(wu_hbm.at[:, cols(c), :], wu_v.at[c], wu_sem.at[c])
        for c in range(chunks)
    ]
    wd_copies = [
        pltpu.make_async_copy(wd_hbm.at[:, :, cols(c)], wd_v.at[c], wd_sem.at[c])
        for c in range(chunks)
    ]
    smalls[0].start()
    wo_copies[0].start()
    for copy in smalls[1:]:
        copy.start()
    for copy in wo_copies[1:]:
        copy.start()
    for c in range(chunks):
        wg_copies[c].start()
        wu_copies[c].start()
    for copy in wd_copies:
        copy.start()

    def wait_bytes(ref, sem):
        pltpu.make_async_copy(ref, ref, sem).wait()

    def to_sibling(stage, c, src, dst):
        pltpu.make_async_remote_copy(
            src_ref=src, dst_ref=dst, send_sem=stage_send.at[stage, c],
            recv_sem=stage_recv.at[stage, c], device_id=sibling, device_id_type=MESH,
        ).start()

    def to_owners(stage, c, src, dst):
        for offset in range(1, chips):
            pltpu.make_async_remote_copy(
                src_ref=src.at[offset - 1], dst_ref=dst.at[offset - 1],
                send_sem=stage_send.at[stage, c], recv_sem=stage_recv.at[stage, c],
                device_id=device(place - offset, low), device_id_type=MESH,
            ).start()

    def to_chips(stage, c, block):
        for offset in range(1, chips):
            pltpu.make_async_remote_copy(
                src_ref=block.at[0], dst_ref=block.at[offset],
                send_sem=stage_send.at[stage, c], recv_sem=stage_recv.at[stage, c],
                device_id=device(place + offset, low), device_id_type=MESH,
            ).start()

    def peers(block):
        return block.at[pl.ds(1, chips - 1)]

    smalls[0].wait()
    attn_blocks[...] = attn_v[...].astype(F32).reshape(attn_blocks.shape)
    picked = []
    for side in (low, 1 - low):
        for offset in range(chips):
            position = lax.rem(place - offset + chips, chips)
            owner = (lax.div(position, tensors) * 2 + side) * tensors + lax.rem(position, tensors)
            picked.append(attn_blocks[owner])
    attn_p[...] = jnp.concatenate(picked, axis=0).astype(BF16)

    def split(product, keep, send):
        keep[...] = product[:half].reshape(chips, rows, width)
        send[...] = product[half:].reshape(chips, rows, width).astype(BF16)

    def project(c):
        wo_copies[c].wait()
        product = jnp.dot(attn_p[...], wo_v[c], preferred_element_type=F32)
        split(product, keep1.at[c], send1.at[c])
        if c == 0:
            pl.semaphore_wait(barrier, chips)
        to_sibling(0, c, send1.at[c], recv1.at[c])
        if c == chunks - 1:
            routing_table()

    def add_sibling(c):
        wait_bytes(recv1.at[c], stage_recv.at[0, c])
        total = keep1[c] + recv1[c].astype(F32)
        own2[c] = total[0]
        send2[c] = total[1:].astype(BF16)
        to_owners(1, c, send2.at[c], recv2.at[c])

    def finish_hidden(c):
        wait_bytes(recv2.at[c], stage_recv.at[1, c])
        total = own2[c] + jnp.sum(recv2[c].astype(F32), axis=0)
        here = slice(c * width, (c + 1) * width)
        projected = total.astype(BF16).astype(F32)
        hidden = (res_v[:, here].astype(F32) + projected).astype(BF16).astype(F32)
        hidden_v[c] = hidden
        square_v[...] = hidden * hidden if c == 0 else square_v[...] + hidden * hidden
        rows_own[c, 0] = (hidden * gain_v[here][None]).astype(BF16)
        to_chips(2, c, rows_own.at[c])
        if c == chunks - 1:
            send_meta()

    def routing_table():
        for copy in smalls[1:]:
            copy.wait()
        lane = lax.broadcasted_iota(jnp.int32, (rows, META), 1).astype(F32)
        square = (rows, rows)
        diagonal = lax.broadcasted_iota(jnp.int32, square, 0) == lax.broadcasted_iota(jnp.int32, square, 1)
        ids = ids_v[...].astype(F32)
        weights = gw_v[...].astype(F32)
        block = jnp.zeros((rows, META), F32)
        for k in range(ids.shape[0]):
            expert = jnp.sum(jnp.where(diagonal, ids[k : k + 1], 0.0), axis=1, keepdims=True)
            weight = jnp.sum(jnp.where(diagonal, weights[k : k + 1], 0.0), axis=1, keepdims=True)
            block = block + jnp.where(lane == expert, weight, 0.0)
        table_v[...] = block

    def send_meta():
        mean = jnp.sum(square_v[...], axis=1, keepdims=True) / (chunks * width)
        scale = lax.rsqrt(mean + 1e-06)
        lane = lax.broadcasted_iota(jnp.int32, (rows, META), 1)
        meta_own[0] = jnp.where(lane == experts_all, scale, table_v[...])
        to_chips(2, chunks, meta_own)

    def forward(c):
        wait_bytes(peers(rows_own.at[c]), stage_recv.at[2, c])
        to_sibling(3, c, rows_own.at[c], rows_sib.at[c])
        if c == chunks - 1:
            wait_bytes(peers(meta_own), stage_recv.at[2, chunks])
            to_sibling(3, chunks, meta_own, meta_sib)

    def experts(c):
        wg_copies[c].wait()
        wu_copies[c].wait()
        wait_bytes(rows_sib.at[c], stage_recv.at[3, c])
        both = jnp.concatenate(
            [rows_own[c].astype(F32).reshape(half, width), rows_sib[c].astype(F32).reshape(half, width)],
            axis=0,
        ).astype(BF16)
        for member in range(members):
            gate = jnp.dot(both, wg_v[c, member], preferred_element_type=F32)
            up = jnp.dot(both, wu_v[c, member], preferred_element_type=F32)
            acc_gate[member] = gate if c == 0 else acc_gate[member] + gate
            acc_up[member] = up if c == 0 else acc_up[member] + up

    def activate():
        wait_bytes(meta_sib, stage_recv.at[3, chunks])
        block = jnp.concatenate([meta_own[...].reshape(half, META), meta_sib[...].reshape(half, META)], axis=0)
        lane = lax.broadcasted_iota(jnp.int32, block.shape, 1)
        scale = block[:, experts_all : experts_all + 1]
        for member in range(members):
            weight = jnp.sum(
                jnp.where(lane == group * members + member, block, 0.0), axis=1, keepdims=True
            )
            gate = acc_gate[member] * scale
            up = acc_up[member] * scale
            act_v[member] = (gate / (1.0 + jnp.exp(-gate)) * up * weight).astype(BF16)

    def down(c):
        wd_copies[c].wait()
        product = jnp.dot(act_v[0], wd_v[c, 0], preferred_element_type=F32)
        for member in range(1, members):
            product = product + jnp.dot(act_v[member], wd_v[c, member], preferred_element_type=F32)
        split(product, keep4.at[c], send4.at[c])
        to_sibling(4, c, send4.at[c], recv4.at[c])

    def add_sibling_down(c):
        wait_bytes(recv4.at[c], stage_recv.at[4, c])
        total = keep4[c] + recv4[c].astype(F32)
        own5[c] = total[0]
        send5[c] = total[1:].astype(BF16)
        to_owners(5, c, send5.at[c], recv5.at[c])

    def finish(c):
        wait_bytes(recv5.at[c], stage_recv.at[5, c])
        total = own5[c] + jnp.sum(recv5[c].astype(F32), axis=0)
        out_v[c] = (hidden_v[c] + total).astype(BF16)
        pltpu.make_async_copy(out_v.at[c], out_hbm.at[:, cols(c)], out_sem.at[c]).start()

    def pipeline(stages):
        steps = [(c + LAGS[s], s, c, stage) for s, stage in enumerate(stages) for c in range(chunks)]
        for _, _, c, stage in sorted(steps, key=lambda step: step[:3]):
            stage(c)

    pipeline([project, add_sibling, finish_hidden, forward, experts])
    activate()
    pipeline([down, add_sibling_down, finish])

    for c in range(chunks):
        pltpu.make_async_copy(out_v.at[c], out_hbm.at[:, cols(c)], out_sem.at[c]).wait()
        wait_bytes(send1.at[c], stage_send.at[0, c])
        wait_bytes(send2.at[c], stage_send.at[1, c])
        wait_bytes(peers(rows_own.at[c]), stage_send.at[2, c])
        wait_bytes(rows_own.at[c], stage_send.at[3, c])
        wait_bytes(send4.at[c], stage_send.at[4, c])
        wait_bytes(send5.at[c], stage_send.at[5, c])
    wait_bytes(peers(meta_own), stage_send.at[2, chunks])
    wait_bytes(meta_own, stage_send.at[3, chunks])


def on_device(
    attn_heads, out_proj, residual_in, norm_gain, expert_ids, gate_weights, w_gate, w_up, w_down
):
    rows, features = residual_in.shape
    tokens, heads = attn_heads.shape
    groups = lax.axis_size("group")
    tensors = lax.axis_size("tensor")
    members, _, units = w_gate.shape
    chips = groups // 2 * tensors
    experts_all = groups * members
    chunks = column_chunks(features)
    width = features // chunks
    dims = (chunks, width, chips, tensors, rows, members, experts_all)

    def vmem(shape, dtype):
        return pltpu.VMEM(shape, dtype)

    exchange = [
        vmem((chunks, chips, rows, width), F32),
        vmem((chunks, chips, rows, width), BF16),
        vmem((chunks, chips, rows, width), BF16),
        vmem((chunks, rows, width), F32),
        vmem((chunks, chips - 1, rows, width), BF16),
        vmem((chunks, chips - 1, rows, width), BF16),
    ]
    scratch = [
        vmem((tokens, heads), BF16),
        vmem((tokens // rows, rows, heads), F32),
        vmem((tokens, heads), BF16),
        vmem((rows, features), BF16),
        vmem((features,), F32),
        vmem(expert_ids.shape[::-1], expert_ids.dtype),
        vmem(gate_weights.shape[::-1], gate_weights.dtype),
        vmem((chunks, heads, width), BF16),
        vmem((chunks, members, width, units), BF16),
        vmem((chunks, members, width, units), BF16),
        vmem((chunks, members, units, width), BF16),
        *exchange,
        vmem((chunks, rows, width), F32),
        vmem((rows, width), F32),
        vmem((rows, META), F32),
        vmem((chunks, chips, rows, width), BF16),
        vmem((chunks, chips, rows, width), BF16),
        vmem((chips, rows, META), F32),
        vmem((chips, rows, META), F32),
        vmem((members, tokens, units), F32),
        vmem((members, tokens, units), F32),
        vmem((members, tokens, units), BF16),
        *exchange,
        vmem((chunks, rows, width), BF16),
        pltpu.SemaphoreType.DMA((5,)),
        pltpu.SemaphoreType.DMA((chunks,)),
        pltpu.SemaphoreType.DMA((chunks,)),
        pltpu.SemaphoreType.DMA((chunks,)),
        pltpu.SemaphoreType.DMA((chunks,)),
        pltpu.SemaphoreType.DMA((chunks,)),
        pltpu.SemaphoreType.DMA((6, chunks + 1)),
        pltpu.SemaphoreType.DMA((6, chunks + 1)),
    ]
    weights = out_proj.size + w_gate.size + w_up.size + w_down.size
    return pl.pallas_call(
        functools.partial(kernel, dims),
        out_shape=jax.ShapeDtypeStruct((rows, features), BF16),
        in_specs=[pl.BlockSpec(memory_space=pl.ANY)] * 9,
        out_specs=pl.BlockSpec(memory_space=pl.ANY),
        scratch_shapes=scratch,
        cost_estimate=pl.CostEstimate(
            flops=2 * tokens * weights, bytes_accessed=2 * weights, transcendentals=0
        ),
        compiler_params=pltpu.CompilerParams(
            collective_id=0, has_side_effects=True, vmem_limit_bytes=56 * 1024 * 1024
        ),
        name="projected_experts",
    )(
        attn_heads, out_proj, residual_in, norm_gain,
        expert_ids.T, gate_weights.T, w_gate, w_up, w_down,
    )


def solution(mesh):
    placed = (
        P("dp", ("group", "tensor")),
        P(("group", "tensor"), None),
        P(("dp", "group", "tensor"), None),
        P(),
        P(("dp", "group", "tensor"), None),
        P(("dp", "group", "tensor"), None),
        P("group", None, "tensor"),
        P("group", None, "tensor"),
        P("group", "tensor", None),
    )
    return jax.shard_map(
        on_device,
        mesh=mesh,
        in_specs=placed,
        out_specs=P(("dp", "group", "tensor"), None),
        check_vma=False,
    )
```

```python
import functools

import jax
import jax.numpy as jnp
from jax import lax
from jax.experimental import pallas as pl
from jax.experimental.pallas import tpu as pltpu
from jax.sharding import PartitionSpec as P

MESH = pl.DeviceIdType.MESH
F32 = jnp.float32
BF16 = jnp.bfloat16
UNITS = 4
META = 128
LAGS = (0, 4, 10, 17, 21)


def column_chunks(features, units, first_short):
    tile = 256 if features % 256 == 0 else 128
    count = features // tile
    sizes = [units] * (count // units) + ([count % units] if count % units else [])
    if first_short:
        sizes = sizes[::-1]
    starts = [sum(sizes[:i]) for i in range(len(sizes))]
    return tuple((start * tile, size * tile) for start, size in zip(starts, sizes))


def kernel(
    dims,
    attn_hbm, wo_hbm, res_hbm, gain_hbm, ids_hbm, gw_hbm, wg_hbm, wu_hbm, wd_hbm,
    out_hbm,
    attn_v, attn_blocks, attn_p, res_v, gain_v, ids_v, gw_v,
    wo_v, wg_v, wu_v, wd_v,
    keep1, send1, recv1, own2, send2, recv2, hidden_v, table_v,
    rows_own, rows_sib, meta_own, meta_sib,
    acc_gate, acc_up, act_v,
    keep4, send4, recv4, own5, send5, recv5, out_v,
    small_sem, wo_sem, wg_sem, wu_sem, wd_sem, out_sem,
    stage_send, stage_recv,
):
    spans, down_spans, chips, tensors, rows, members, experts_all = dims
    chunks, down_chunks = len(spans), len(down_spans)
    features = res_v.shape[1]
    half = chips * rows
    group, tensor = lax.axis_index("group"), lax.axis_index("tensor")
    high, low = lax.div(group, 2), lax.rem(group, 2)
    place = high * tensors + tensor

    def device(position, side):
        position = lax.rem(position + chips, chips)
        return {"group": lax.div(position, tensors) * 2 + side, "tensor": lax.rem(position, tensors)}

    sibling = {"group": high * 2 + 1 - low, "tensor": tensor}

    barrier = pltpu.get_barrier_semaphore()
    pl.semaphore_signal(barrier, inc=1, device_id=sibling, device_id_type=MESH)
    for offset in range(1, chips):
        pl.semaphore_signal(
            barrier, inc=1, device_id=device(place + offset, low), device_id_type=MESH
        )

    def part(ref, span, axis=-1):
        index = [slice(None)] * len(ref.shape)
        index[axis] = pl.ds(*span)
        return ref.at[tuple(index)]

    smalls = [
        pltpu.make_async_copy(src, dst, small_sem.at[i])
        for i, (src, dst) in enumerate(
            [(attn_hbm, attn_v), (res_hbm, res_v), (gain_hbm, gain_v), (ids_hbm, ids_v), (gw_hbm, gw_v)]
        )
    ]
    def fetches(src, dst, sems, pieces, axis):
        return [
            pltpu.make_async_copy(part(src, span, axis), part(dst, span, axis), sems.at[c])
            for c, span in enumerate(pieces)
        ]

    wo_copies = fetches(wo_hbm, wo_v, wo_sem, spans, 1)
    wg_copies = fetches(wg_hbm, wg_v, wg_sem, spans, 1)
    wu_copies = fetches(wu_hbm, wu_v, wu_sem, spans, 1)
    wd_copies = fetches(wd_hbm, wd_v, wd_sem, down_spans, 2)
    smalls[0].start()
    wo_copies[0].start()
    for copy in smalls[1:]:
        copy.start()
    for copy in wo_copies[1:]:
        copy.start()
    for c in range(chunks):
        wg_copies[c].start()
        wu_copies[c].start()
    for copy in wd_copies:
        copy.start()

    def wait_bytes(ref, sem):
        pltpu.make_async_copy(ref, ref, sem).wait()

    def to_sibling(stage, c, src, dst):
        pltpu.make_async_remote_copy(
            src_ref=src, dst_ref=dst, send_sem=stage_send.at[stage, c],
            recv_sem=stage_recv.at[stage, c], device_id=sibling, device_id_type=MESH,
        ).start()

    def to_owners(stage, c, src, dst):
        for offset in range(1, chips):
            pltpu.make_async_remote_copy(
                src_ref=src.at[offset - 1], dst_ref=dst.at[offset - 1],
                send_sem=stage_send.at[stage, c], recv_sem=stage_recv.at[stage, c],
                device_id=device(place - offset, low), device_id_type=MESH,
            ).start()

    def to_chips(stage, c, block):
        for offset in range(1, chips):
            pltpu.make_async_remote_copy(
                src_ref=block.at[0], dst_ref=block.at[offset],
                send_sem=stage_send.at[stage, c], recv_sem=stage_recv.at[stage, c],
                device_id=device(place + offset, low), device_id_type=MESH,
            ).start()

    def peers(block):
        return block.at[pl.ds(1, chips - 1)]

    smalls[0].wait()
    attn_blocks[...] = attn_v[...].astype(F32).reshape(attn_blocks.shape)
    picked = []
    for side in (low, 1 - low):
        for offset in range(chips):
            position = lax.rem(place - offset + chips, chips)
            owner = (lax.div(position, tensors) * 2 + side) * tensors + lax.rem(position, tensors)
            picked.append(attn_blocks[owner])
    attn_p[...] = jnp.concatenate(picked, axis=0).astype(BF16)

    def split(product, keep, send):
        width = product.shape[1]
        keep[...] = product[:half].reshape(chips, rows, width)
        send[...] = product[half:].reshape(chips, rows, width).astype(BF16)

    def project(c, span):
        wo_copies[c].wait()
        product = jnp.dot(attn_p[...], part(wo_v, span)[...], preferred_element_type=F32)
        split(product, part(keep1, span), part(send1, span))
        if c == 0:
            pl.semaphore_wait(barrier, chips)
        to_sibling(0, c, part(send1, span), part(recv1, span))
        if c == chunks - 1:
            routing_table()

    def add_sibling(c, span):
        wait_bytes(part(recv1, span), stage_recv.at[0, c])
        total = part(keep1, span)[...] + part(recv1, span)[...].astype(F32)
        part(own2, span)[...] = total[0]
        part(send2, span)[...] = total[1:].astype(BF16)
        to_owners(1, c, part(send2, span), part(recv2, span))

    squares = []

    def finish_hidden(c, span):
        wait_bytes(part(recv2, span), stage_recv.at[1, c])
        total = part(own2, span)[...] + jnp.sum(part(recv2, span)[...].astype(F32), axis=0)
        projected = total.astype(BF16).astype(F32)
        hidden = (part(res_v, span)[...].astype(F32) + projected).astype(BF16).astype(F32)
        part(hidden_v, span)[...] = hidden
        part(rows_own, span)[0] = (hidden * part(gain_v, span)[...][None]).astype(BF16)
        to_chips(2, c, part(rows_own, span))
        squares.append(jnp.sum(hidden * hidden, axis=1, keepdims=True))
        if c == chunks - 1:
            send_meta()

    def routing_table():
        for copy in smalls[1:]:
            copy.wait()
        lane = lax.broadcasted_iota(jnp.int32, (rows, META), 1).astype(F32)
        square = (rows, rows)
        diagonal = lax.broadcasted_iota(jnp.int32, square, 0) == lax.broadcasted_iota(jnp.int32, square, 1)
        ids = ids_v[...].astype(F32)
        weights = gw_v[...].astype(F32)
        block = jnp.zeros((rows, META), F32)
        for k in range(ids.shape[0]):
            expert = jnp.sum(jnp.where(diagonal, ids[k : k + 1], 0.0), axis=1, keepdims=True)
            weight = jnp.sum(jnp.where(diagonal, weights[k : k + 1], 0.0), axis=1, keepdims=True)
            block = block + jnp.where(lane == expert, weight, 0.0)
        table_v[...] = block

    def send_meta():
        mean = sum(squares[1:], squares[0]) / features
        scale = lax.rsqrt(mean + 1e-06)
        lane = lax.broadcasted_iota(jnp.int32, (rows, META), 1)
        meta_own[0] = jnp.where(lane == experts_all, scale, table_v[...])
        to_chips(2, chunks, meta_own)

    def forward(c, span):
        wait_bytes(peers(part(rows_own, span)), stage_recv.at[2, c])
        to_sibling(3, c, part(rows_own, span), part(rows_sib, span))
        if c == chunks - 1:
            wait_bytes(peers(meta_own), stage_recv.at[2, chunks])
            to_sibling(3, chunks, meta_own, meta_sib)

    def experts(c, span):
        wg_copies[c].wait()
        wu_copies[c].wait()
        wait_bytes(part(rows_sib, span), stage_recv.at[3, c])
        both = jnp.concatenate(
            [part(ref, span)[...].astype(F32).reshape(half, span[1]) for ref in (rows_own, rows_sib)], axis=0
        ).astype(BF16)
        for member in range(members):
            gate = jnp.dot(both, part(wg_v, span, 1)[member], preferred_element_type=F32)
            up = jnp.dot(both, part(wu_v, span, 1)[member], preferred_element_type=F32)
            acc_gate[member] = gate if c == 0 else acc_gate[member] + gate
            acc_up[member] = up if c == 0 else acc_up[member] + up

    def activate():
        wait_bytes(meta_sib, stage_recv.at[3, chunks])
        block = jnp.concatenate([meta_own[...].reshape(half, META), meta_sib[...].reshape(half, META)], axis=0)
        lane = lax.broadcasted_iota(jnp.int32, block.shape, 1)
        scale = block[:, experts_all : experts_all + 1]
        for member in range(members):
            weight = jnp.sum(
                jnp.where(lane == group * members + member, block, 0.0), axis=1, keepdims=True
            )
            gate = acc_gate[member] * scale
            up = acc_up[member] * scale
            act_v[member] = (gate / (1.0 + jnp.exp(-gate)) * up * weight).astype(BF16)

    def down(c, span):
        wd_copies[c].wait()
        product = jnp.dot(act_v[0], part(wd_v, span)[0], preferred_element_type=F32)
        for member in range(1, members):
            product = product + jnp.dot(act_v[member], part(wd_v, span)[member], preferred_element_type=F32)
        split(product, part(keep4, span), part(send4, span))
        to_sibling(4, c, part(send4, span), part(recv4, span))

    def add_sibling_down(c, span):
        wait_bytes(part(recv4, span), stage_recv.at[4, c])
        total = part(keep4, span)[...] + part(recv4, span)[...].astype(F32)
        part(own5, span)[...] = total[0]
        part(send5, span)[...] = total[1:].astype(BF16)
        to_owners(5, c, part(send5, span), part(recv5, span))

    def write_out(c, span):
        return pltpu.make_async_copy(part(out_v, span), part(out_hbm, span), out_sem.at[c])

    def finish(c, span):
        wait_bytes(part(recv5, span), stage_recv.at[5, c])
        total = part(own5, span)[...] + jnp.sum(part(recv5, span)[...].astype(F32), axis=0)
        part(out_v, span)[...] = (part(hidden_v, span)[...] + total).astype(BF16)
        write_out(c, span).start()

    def pipeline(stages, pieces):
        unit = features / 7
        steps = [
            ((span[0] + span[1]) / unit + LAGS[s], s, c, stage)
            for s, stage in enumerate(stages)
            for c, span in enumerate(pieces)
        ]
        for _, _, c, stage in sorted(steps, key=lambda step: step[:3]):
            stage(c, pieces[c])

    pipeline([project, add_sibling, finish_hidden, forward, experts], spans)
    activate()
    pipeline([down, add_sibling_down, finish], down_spans)

    for c, span in enumerate(spans):
        wait_bytes(part(send1, span), stage_send.at[0, c])
        wait_bytes(part(send2, span), stage_send.at[1, c])
        wait_bytes(peers(part(rows_own, span)), stage_send.at[2, c])
        wait_bytes(part(rows_own, span), stage_send.at[3, c])
    for c, span in enumerate(down_spans):
        wait_bytes(part(send4, span), stage_send.at[4, c])
        wait_bytes(part(send5, span), stage_send.at[5, c])
        write_out(c, span).wait()
    wait_bytes(peers(meta_own), stage_send.at[2, chunks])
    wait_bytes(meta_own, stage_send.at[3, chunks])


def on_device(
    attn_heads, out_proj, residual_in, norm_gain, expert_ids, gate_weights, w_gate, w_up, w_down
):
    rows, features = residual_in.shape
    tokens, heads = attn_heads.shape
    groups = lax.axis_size("group")
    tensors = lax.axis_size("tensor")
    members, _, units = w_gate.shape
    chips = groups // 2 * tensors
    experts_all = groups * members
    spans = column_chunks(features, UNITS, True)
    down_spans = column_chunks(features, UNITS, False)
    chunks = max(len(spans), len(down_spans))
    dims = (spans, down_spans, chips, tensors, rows, members, experts_all)

    def vmem(shape, dtype):
        return pltpu.VMEM(shape, dtype)

    exchange = [
        vmem((chips, rows, features), F32),
        vmem((chips, rows, features), BF16),
        vmem((chips, rows, features), BF16),
        vmem((rows, features), F32),
        vmem((chips - 1, rows, features), BF16),
        vmem((chips - 1, rows, features), BF16),
    ]
    scratch = [
        vmem((tokens, heads), BF16),
        vmem((tokens // rows, rows, heads), F32),
        vmem((tokens, heads), BF16),
        vmem((rows, features), BF16),
        vmem((features,), F32),
        vmem(expert_ids.shape[::-1], expert_ids.dtype),
        vmem(gate_weights.shape[::-1], gate_weights.dtype),
        vmem((heads, features), BF16),
        vmem((members, features, units), BF16),
        vmem((members, features, units), BF16),
        vmem((members, units, features), BF16),
        *exchange,
        vmem((rows, features), F32),
        vmem((rows, META), F32),
        vmem((chips, rows, features), BF16),
        vmem((chips, rows, features), BF16),
        vmem((chips, rows, META), F32),
        vmem((chips, rows, META), F32),
        vmem((members, tokens, units), F32),
        vmem((members, tokens, units), F32),
        vmem((members, tokens, units), BF16),
        *exchange,
        vmem((rows, features), BF16),
        pltpu.SemaphoreType.DMA((5,)),
        pltpu.SemaphoreType.DMA((chunks,)),
        pltpu.SemaphoreType.DMA((chunks,)),
        pltpu.SemaphoreType.DMA((chunks,)),
        pltpu.SemaphoreType.DMA((chunks,)),
        pltpu.SemaphoreType.DMA((chunks,)),
        pltpu.SemaphoreType.DMA((6, chunks + 1)),
        pltpu.SemaphoreType.DMA((6, chunks + 1)),
    ]
    weights = out_proj.size + w_gate.size + w_up.size + w_down.size
    return pl.pallas_call(
        functools.partial(kernel, dims),
        out_shape=jax.ShapeDtypeStruct((rows, features), BF16),
        in_specs=[pl.BlockSpec(memory_space=pl.ANY)] * 9,
        out_specs=pl.BlockSpec(memory_space=pl.ANY),
        scratch_shapes=scratch,
        cost_estimate=pl.CostEstimate(
            flops=2 * tokens * weights, bytes_accessed=2 * weights, transcendentals=0
        ),
        compiler_params=pltpu.CompilerParams(
            collective_id=0, has_side_effects=True, vmem_limit_bytes=56 * 1024 * 1024
        ),
        name="projected_experts",
    )(
        attn_heads, out_proj, residual_in, norm_gain,
        expert_ids.T, gate_weights.T, w_gate, w_up, w_down,
    )


def solution(mesh):
    placed = (
        P("dp", ("group", "tensor")),
        P(("group", "tensor"), None),
        P(("dp", "group", "tensor"), None),
        P(),
        P(("dp", "group", "tensor"), None),
        P(("dp", "group", "tensor"), None),
        P("group", None, "tensor"),
        P("group", None, "tensor"),
        P("group", "tensor", None),
    )
    return jax.shard_map(
        on_device,
        mesh=mesh,
        in_specs=placed,
        out_specs=P(("dp", "group", "tensor"), None),
        check_vma=False,
    )
```

```python
import functools

import jax
import jax.numpy as jnp
from jax import lax
from jax.experimental import pallas as pl
from jax.experimental.pallas import tpu as pltpu
from jax.sharding import PartitionSpec as P

MESH = pl.DeviceIdType.MESH
F32 = jnp.float32
BF16 = jnp.bfloat16
UNITS = 2
META = 128
LAGS = (0, 4, 10, 17, 21)


def column_chunks(features, units, first_short):
    tile = 256 if features % 256 == 0 else 128
    count = features // tile
    sizes = [units] * (count // units) + ([count % units] if count % units else [])
    if first_short:
        sizes = sizes[::-1]
    starts = [sum(sizes[:i]) for i in range(len(sizes))]
    return tuple((start * tile, size * tile) for start, size in zip(starts, sizes))


def kernel(
    dims,
    attn_hbm, wo_hbm, res_hbm, gain_hbm, ids_hbm, gw_hbm, wg_hbm, wu_hbm, wd_hbm,
    out_hbm,
    attn_v, attn_blocks, attn_p, res_v, gain_v, ids_v, gw_v,
    wo_v, wg_v, wu_v, wd_v,
    keep1, send1, recv1, own2, send2, recv2, hidden_v, table_v,
    rows_own, rows_sib, meta_own, meta_sib,
    acc_gate, acc_up, act_v,
    keep4, send4, recv4, own5, send5, recv5, out_v,
    small_sem, wo_sem, wg_sem, wu_sem, wd_sem, out_sem,
    stage_send, stage_recv,
):
    spans, down_spans, chips, tensors, rows, members, experts_all = dims
    chunks, down_chunks = len(spans), len(down_spans)
    features = res_v.shape[1]
    half = chips * rows
    group, tensor = lax.axis_index("group"), lax.axis_index("tensor")
    high, low = lax.div(group, 2), lax.rem(group, 2)
    place = high * tensors + tensor

    def device(position, side):
        position = lax.rem(position + chips, chips)
        return {"group": lax.div(position, tensors) * 2 + side, "tensor": lax.rem(position, tensors)}

    sibling = {"group": high * 2 + 1 - low, "tensor": tensor}

    barrier = pltpu.get_barrier_semaphore()
    pl.semaphore_signal(barrier, inc=1, device_id=sibling, device_id_type=MESH)
    for offset in range(1, chips):
        pl.semaphore_signal(
            barrier, inc=1, device_id=device(place + offset, low), device_id_type=MESH
        )

    def part(ref, span, axis=-1):
        index = [slice(None)] * len(ref.shape)
        index[axis] = pl.ds(*span)
        return ref.at[tuple(index)]

    smalls = [
        pltpu.make_async_copy(src, dst, small_sem.at[i])
        for i, (src, dst) in enumerate(
            [(attn_hbm, attn_v), (res_hbm, res_v), (gain_hbm, gain_v), (ids_hbm, ids_v), (gw_hbm, gw_v)]
        )
    ]
    def fetches(src, dst, sems, pieces, axis):
        return [
            pltpu.make_async_copy(part(src, span, axis), part(dst, span, axis), sems.at[c])
            for c, span in enumerate(pieces)
        ]

    wo_copies = fetches(wo_hbm, wo_v, wo_sem, spans, 1)
    wg_copies = fetches(wg_hbm, wg_v, wg_sem, spans, 1)
    wu_copies = fetches(wu_hbm, wu_v, wu_sem, spans, 1)
    wd_copies = fetches(wd_hbm, wd_v, wd_sem, down_spans, 2)
    queue = list(wo_copies)
    for gate_copy, up_copy in zip(wg_copies, wu_copies):
        queue += [gate_copy, up_copy]
    queue += wd_copies

    def fetch_more(count):
        for _ in range(min(count, len(queue))):
            queue.pop(0).start()

    def need(copy):
        while any(copy is later for later in queue):
            fetch_more(1)
        copy.wait()

    smalls[0].start()
    fetch_more(1)
    for copy in smalls[1:]:
        copy.start()
    fetch_more(2)

    def wait_bytes(ref, sem):
        pltpu.make_async_copy(ref, ref, sem).wait()

    def to_sibling(stage, c, src, dst):
        pltpu.make_async_remote_copy(
            src_ref=src, dst_ref=dst, send_sem=stage_send.at[stage, c],
            recv_sem=stage_recv.at[stage, c], device_id=sibling, device_id_type=MESH,
        ).start()

    def to_owners(stage, c, src, dst):
        for offset in range(1, chips):
            pltpu.make_async_remote_copy(
                src_ref=src.at[offset - 1], dst_ref=dst.at[offset - 1],
                send_sem=stage_send.at[stage, c], recv_sem=stage_recv.at[stage, c],
                device_id=device(place - offset, low), device_id_type=MESH,
            ).start()

    def to_chips(stage, c, block):
        for offset in range(1, chips):
            pltpu.make_async_remote_copy(
                src_ref=block.at[0], dst_ref=block.at[offset],
                send_sem=stage_send.at[stage, c], recv_sem=stage_recv.at[stage, c],
                device_id=device(place + offset, low), device_id_type=MESH,
            ).start()

    def peers(block):
        return block.at[pl.ds(1, chips - 1)]

    smalls[0].wait()
    attn_blocks[...] = attn_v[...].astype(F32).reshape(attn_blocks.shape)
    picked = []
    for side in (low, 1 - low):
        for offset in range(chips):
            position = lax.rem(place - offset + chips, chips)
            owner = (lax.div(position, tensors) * 2 + side) * tensors + lax.rem(position, tensors)
            picked.append(attn_blocks[owner])
    attn_p[...] = jnp.concatenate(picked, axis=0).astype(BF16)

    def split(product, keep, send):
        width = product.shape[1]
        keep[...] = product[:half].reshape(chips, rows, width)
        send[...] = product[half:].reshape(chips, rows, width).astype(BF16)

    def project(c, span):
        need(wo_copies[c])
        product = jnp.dot(attn_p[...], part(wo_v, span)[...], preferred_element_type=F32)
        split(product, part(keep1, span), part(send1, span))
        if c == 0:
            pl.semaphore_wait(barrier, chips)
        to_sibling(0, c, part(send1, span), part(recv1, span))
        if c == chunks - 1:
            routing_table()

    def add_sibling(c, span):
        wait_bytes(part(recv1, span), stage_recv.at[0, c])
        total = part(keep1, span)[...] + part(recv1, span)[...].astype(F32)
        part(own2, span)[...] = total[0]
        part(send2, span)[...] = total[1:].astype(BF16)
        to_owners(1, c, part(send2, span), part(recv2, span))

    squares = []

    def finish_hidden(c, span):
        wait_bytes(part(recv2, span), stage_recv.at[1, c])
        total = part(own2, span)[...] + jnp.sum(part(recv2, span)[...].astype(F32), axis=0)
        projected = total.astype(BF16).astype(F32)
        hidden = (part(res_v, span)[...].astype(F32) + projected).astype(BF16).astype(F32)
        part(hidden_v, span)[...] = hidden
        part(rows_own, span)[0] = (hidden * part(gain_v, span)[...][None]).astype(BF16)
        to_chips(2, c, part(rows_own, span))
        squares.append(jnp.sum(hidden * hidden, axis=1, keepdims=True))
        if c == chunks - 1:
            send_meta()

    def routing_table():
        for copy in smalls[1:]:
            copy.wait()
        lane = lax.broadcasted_iota(jnp.int32, (rows, META), 1).astype(F32)
        square = (rows, rows)
        diagonal = lax.broadcasted_iota(jnp.int32, square, 0) == lax.broadcasted_iota(jnp.int32, square, 1)
        ids = ids_v[...].astype(F32)
        weights = gw_v[...].astype(F32)
        block = jnp.zeros((rows, META), F32)
        for k in range(ids.shape[0]):
            expert = jnp.sum(jnp.where(diagonal, ids[k : k + 1], 0.0), axis=1, keepdims=True)
            weight = jnp.sum(jnp.where(diagonal, weights[k : k + 1], 0.0), axis=1, keepdims=True)
            block = block + jnp.where(lane == expert, weight, 0.0)
        table_v[...] = block

    def send_meta():
        mean = sum(squares[1:], squares[0]) / features
        scale = lax.rsqrt(mean + 1e-06)
        lane = lax.broadcasted_iota(jnp.int32, (rows, META), 1)
        meta_own[0] = jnp.where(lane == experts_all, scale, table_v[...])
        to_chips(2, chunks, meta_own)

    def forward(c, span):
        wait_bytes(peers(part(rows_own, span)), stage_recv.at[2, c])
        to_sibling(3, c, part(rows_own, span), part(rows_sib, span))
        if c == chunks - 1:
            wait_bytes(peers(meta_own), stage_recv.at[2, chunks])
            to_sibling(3, chunks, meta_own, meta_sib)

    def experts(c, span):
        need(wg_copies[c])
        need(wu_copies[c])
        wait_bytes(part(rows_sib, span), stage_recv.at[3, c])
        both = jnp.concatenate(
            [part(ref, span)[...].astype(F32).reshape(half, span[1]) for ref in (rows_own, rows_sib)], axis=0
        ).astype(BF16)
        for member in range(members):
            gate = jnp.dot(both, part(wg_v, span, 1)[member], preferred_element_type=F32)
            up = jnp.dot(both, part(wu_v, span, 1)[member], preferred_element_type=F32)
            acc_gate[member] = gate if c == 0 else acc_gate[member] + gate
            acc_up[member] = up if c == 0 else acc_up[member] + up

    def activate():
        wait_bytes(meta_sib, stage_recv.at[3, chunks])
        block = jnp.concatenate([meta_own[...].reshape(half, META), meta_sib[...].reshape(half, META)], axis=0)
        lane = lax.broadcasted_iota(jnp.int32, block.shape, 1)
        scale = block[:, experts_all : experts_all + 1]
        for member in range(members):
            weight = jnp.sum(
                jnp.where(lane == group * members + member, block, 0.0), axis=1, keepdims=True
            )
            gate = acc_gate[member] * scale
            up = acc_up[member] * scale
            act_v[member] = (gate / (1.0 + jnp.exp(-gate)) * up * weight).astype(BF16)

    def down(c, span):
        need(wd_copies[c])
        product = jnp.dot(act_v[0], part(wd_v, span)[0], preferred_element_type=F32)
        for member in range(1, members):
            product = product + jnp.dot(act_v[member], part(wd_v, span)[member], preferred_element_type=F32)
        split(product, part(keep4, span), part(send4, span))
        to_sibling(4, c, part(send4, span), part(recv4, span))

    def add_sibling_down(c, span):
        wait_bytes(part(recv4, span), stage_recv.at[4, c])
        total = part(keep4, span)[...] + part(recv4, span)[...].astype(F32)
        part(own5, span)[...] = total[0]
        part(send5, span)[...] = total[1:].astype(BF16)
        to_owners(5, c, part(send5, span), part(recv5, span))

    def write_out(c, span):
        return pltpu.make_async_copy(part(out_v, span), part(out_hbm, span), out_sem.at[c])

    def finish(c, span):
        wait_bytes(part(recv5, span), stage_recv.at[5, c])
        total = part(own5, span)[...] + jnp.sum(part(recv5, span)[...].astype(F32), axis=0)
        part(out_v, span)[...] = (part(hidden_v, span)[...] + total).astype(BF16)
        write_out(c, span).start()

    def pipeline(stages, pieces):
        unit = features / 7
        steps = [
            ((span[0] + span[1]) / unit + LAGS[s], s, c, stage)
            for s, stage in enumerate(stages)
            for c, span in enumerate(pieces)
        ]
        for _, _, c, stage in sorted(steps, key=lambda step: step[:3]):
            stage(c, pieces[c])
            fetch_more(1)

    pipeline([project, add_sibling, finish_hidden, forward, experts], spans)
    activate()
    pipeline([down, add_sibling_down, finish], down_spans)

    for c, span in enumerate(spans):
        wait_bytes(part(send1, span), stage_send.at[0, c])
        wait_bytes(part(send2, span), stage_send.at[1, c])
        wait_bytes(peers(part(rows_own, span)), stage_send.at[2, c])
        wait_bytes(part(rows_own, span), stage_send.at[3, c])
    for c, span in enumerate(down_spans):
        wait_bytes(part(send4, span), stage_send.at[4, c])
        wait_bytes(part(send5, span), stage_send.at[5, c])
        write_out(c, span).wait()
    wait_bytes(peers(meta_own), stage_send.at[2, chunks])
    wait_bytes(meta_own, stage_send.at[3, chunks])


def on_device(
    attn_heads, out_proj, residual_in, norm_gain, expert_ids, gate_weights, w_gate, w_up, w_down
):
    rows, features = residual_in.shape
    tokens, heads = attn_heads.shape
    groups = lax.axis_size("group")
    tensors = lax.axis_size("tensor")
    members, _, units = w_gate.shape
    chips = groups // 2 * tensors
    experts_all = groups * members
    spans = column_chunks(features, UNITS, True)
    down_spans = column_chunks(features, UNITS, False)
    chunks = max(len(spans), len(down_spans))
    dims = (spans, down_spans, chips, tensors, rows, members, experts_all)

    def vmem(shape, dtype):
        return pltpu.VMEM(shape, dtype)

    exchange = [
        vmem((chips, rows, features), F32),
        vmem((chips, rows, features), BF16),
        vmem((chips, rows, features), BF16),
        vmem((rows, features), F32),
        vmem((chips - 1, rows, features), BF16),
        vmem((chips - 1, rows, features), BF16),
    ]
    scratch = [
        vmem((tokens, heads), BF16),
        vmem((tokens // rows, rows, heads), F32),
        vmem((tokens, heads), BF16),
        vmem((rows, features), BF16),
        vmem((features,), F32),
        vmem(expert_ids.shape[::-1], expert_ids.dtype),
        vmem(gate_weights.shape[::-1], gate_weights.dtype),
        vmem((heads, features), BF16),
        vmem((members, features, units), BF16),
        vmem((members, features, units), BF16),
        vmem((members, units, features), BF16),
        *exchange,
        vmem((rows, features), F32),
        vmem((rows, META), F32),
        vmem((chips, rows, features), BF16),
        vmem((chips, rows, features), BF16),
        vmem((chips, rows, META), F32),
        vmem((chips, rows, META), F32),
        vmem((members, tokens, units), F32),
        vmem((members, tokens, units), F32),
        vmem((members, tokens, units), BF16),
        *exchange,
        vmem((rows, features), BF16),
        pltpu.SemaphoreType.DMA((5,)),
        pltpu.SemaphoreType.DMA((chunks,)),
        pltpu.SemaphoreType.DMA((chunks,)),
        pltpu.SemaphoreType.DMA((chunks,)),
        pltpu.SemaphoreType.DMA((chunks,)),
        pltpu.SemaphoreType.DMA((chunks,)),
        pltpu.SemaphoreType.DMA((6, chunks + 1)),
        pltpu.SemaphoreType.DMA((6, chunks + 1)),
    ]
    weights = out_proj.size + w_gate.size + w_up.size + w_down.size
    return pl.pallas_call(
        functools.partial(kernel, dims),
        out_shape=jax.ShapeDtypeStruct((rows, features), BF16),
        in_specs=[pl.BlockSpec(memory_space=pl.ANY)] * 9,
        out_specs=pl.BlockSpec(memory_space=pl.ANY),
        scratch_shapes=scratch,
        cost_estimate=pl.CostEstimate(
            flops=2 * tokens * weights, bytes_accessed=2 * weights, transcendentals=0
        ),
        compiler_params=pltpu.CompilerParams(
            collective_id=0, has_side_effects=True, vmem_limit_bytes=56 * 1024 * 1024
        ),
        name="projected_experts",
    )(
        attn_heads, out_proj, residual_in, norm_gain,
        expert_ids.T, gate_weights.T, w_gate, w_up, w_down,
    )


def solution(mesh):
    placed = (
        P("dp", ("group", "tensor")),
        P(("group", "tensor"), None),
        P(("dp", "group", "tensor"), None),
        P(),
        P(("dp", "group", "tensor"), None),
        P(("dp", "group", "tensor"), None),
        P("group", None, "tensor"),
        P("group", None, "tensor"),
        P("group", "tensor", None),
    )
    return jax.shard_map(
        on_device,
        mesh=mesh,
        in_specs=placed,
        out_specs=P(("dp", "group", "tensor"), None),
        check_vma=False,
    )
```

```python
import functools

import jax
import jax.numpy as jnp
from jax import lax
from jax.experimental import pallas as pl
from jax.experimental.pallas import tpu as pltpu
from jax.sharding import PartitionSpec as P

MESH = pl.DeviceIdType.MESH
F32 = jnp.float32
BF16 = jnp.bfloat16
UNITS = 2
META = 128
LAGS = (0, 4, 10, 17, 21)


def column_chunks(features, units, first_short):
    tile = 256 if features % 256 == 0 else 128
    count = features // tile
    sizes = [units] * (count // units) + ([count % units] if count % units else [])
    if first_short:
        sizes = sizes[::-1]
    starts = [sum(sizes[:i]) for i in range(len(sizes))]
    return tuple((start * tile, size * tile) for start, size in zip(starts, sizes))


def kernel(
    dims,
    attn_hbm, wo_hbm, res_hbm, gain_hbm, ids_hbm, gw_hbm, wg_hbm, wu_hbm, wd_hbm,
    out_hbm,
    attn_v, attn_blocks, attn_p, res_v, gain_v, ids_v, gw_v,
    wo_v, wg_v, wu_v, wd_v,
    keep1, send1, recv1, own2, send2, recv2, hidden_v, table_v,
    rows_own, rows_sib, meta_own, meta_sib,
    acc_gate, acc_up, act_v,
    keep4, send4, recv4, own5, send5, recv5, out_v,
    small_sem, wo_sem, wg_sem, wu_sem, wd_sem, out_sem,
    stage_send, stage_recv,
):
    spans, down_spans, chips, tensors, rows, members, experts_all = dims
    chunks, down_chunks = len(spans), len(down_spans)
    features = res_v.shape[1]
    half = chips * rows
    group, tensor = lax.axis_index("group"), lax.axis_index("tensor")
    high, low = lax.div(group, 2), lax.rem(group, 2)
    place = high * tensors + tensor

    def device(position, side):
        position = lax.rem(position + chips, chips)
        return {"group": lax.div(position, tensors) * 2 + side, "tensor": lax.rem(position, tensors)}

    sibling = {"group": high * 2 + 1 - low, "tensor": tensor}

    barrier = pltpu.get_barrier_semaphore()
    pl.semaphore_signal(barrier, inc=1, device_id=sibling, device_id_type=MESH)
    for offset in range(1, chips):
        pl.semaphore_signal(
            barrier, inc=1, device_id=device(place + offset, low), device_id_type=MESH
        )

    def part(ref, span, axis=-1):
        index = [slice(None)] * len(ref.shape)
        index[axis] = pl.ds(*span)
        return ref.at[tuple(index)]

    smalls = [
        pltpu.make_async_copy(src, dst, small_sem.at[i])
        for i, (src, dst) in enumerate(
            [(attn_hbm, attn_v), (res_hbm, res_v), (gain_hbm, gain_v), (ids_hbm, ids_v), (gw_hbm, gw_v)]
        )
    ]
    def fetches(src, dst, sems, pieces, axis):
        return [
            pltpu.make_async_copy(part(src, span, axis), part(dst, span, axis), sems.at[c])
            for c, span in enumerate(pieces)
        ]

    wo_copies = fetches(wo_hbm, wo_v, wo_sem, spans, 1)
    wg_copies = fetches(wg_hbm, wg_v, wg_sem, spans, 1)
    wu_copies = fetches(wu_hbm, wu_v, wu_sem, spans, 1)
    wd_copies = fetches(wd_hbm, wd_v, wd_sem, down_spans, 2)
    queue = list(wo_copies)
    for gate_copy, up_copy in zip(wg_copies, wu_copies):
        queue += [gate_copy, up_copy]
    queue += wd_copies

    def fetch_more(count):
        for _ in range(min(count, len(queue))):
            queue.pop(0).start()

    def need(copy):
        while any(copy is later for later in queue):
            fetch_more(1)
        copy.wait()

    smalls[0].start()
    fetch_more(1)
    for copy in smalls[1:]:
        copy.start()
    fetch_more(2)

    def wait_bytes(ref, sem):
        pltpu.make_async_copy(ref, ref, sem).wait()

    def to_sibling(stage, c, src, dst):
        pltpu.make_async_remote_copy(
            src_ref=src, dst_ref=dst, send_sem=stage_send.at[stage, c],
            recv_sem=stage_recv.at[stage, c], device_id=sibling, device_id_type=MESH,
        ).start()

    def to_owners(stage, c, src, dst):
        for offset in range(1, chips):
            pltpu.make_async_remote_copy(
                src_ref=src.at[offset - 1], dst_ref=dst.at[offset - 1],
                send_sem=stage_send.at[stage, c], recv_sem=stage_recv.at[stage, c],
                device_id=device(place - offset, low), device_id_type=MESH,
            ).start()

    def to_chips(stage, c, block):
        for offset in range(1, chips):
            pltpu.make_async_remote_copy(
                src_ref=block.at[0], dst_ref=block.at[offset],
                send_sem=stage_send.at[stage, c], recv_sem=stage_recv.at[stage, c],
                device_id=device(place + offset, low), device_id_type=MESH,
            ).start()

    def peers(block):
        return block.at[pl.ds(1, chips - 1)]

    smalls[0].wait()
    attn_blocks[...] = attn_v[...].astype(F32).reshape(attn_blocks.shape)
    picked = []
    for side in (low, 1 - low):
        for offset in range(chips):
            position = lax.rem(place - offset + chips, chips)
            owner = (lax.div(position, tensors) * 2 + side) * tensors + lax.rem(position, tensors)
            picked.append(attn_blocks[owner])
    attn_p[...] = jnp.concatenate(picked, axis=0).astype(BF16)

    def split(product, keep, send):
        width = product.shape[1]
        keep[...] = product[:half].reshape(chips, rows, width)
        send[...] = product[half:].reshape(chips, rows, width).astype(BF16)

    def project(c, span):
        need(wo_copies[c])
        product = jnp.dot(attn_p[...], part(wo_v, span)[...], preferred_element_type=F32)
        split(product, part(keep1, span), part(send1, span))
        if c == 0:
            pl.semaphore_wait(barrier, chips)
        to_sibling(0, c, part(send1, span), part(recv1, span))
        if c == chunks - 1:
            routing_table()

    def add_sibling(c, span):
        wait_bytes(part(recv1, span), stage_recv.at[0, c])
        total = part(keep1, span)[...] + part(recv1, span)[...].astype(F32)
        part(own2, span)[...] = total[0]
        part(send2, span)[...] = total[1:].astype(BF16)
        to_owners(1, c, part(send2, span), part(recv2, span))

    squares = []

    def finish_hidden(c, span):
        wait_bytes(part(recv2, span), stage_recv.at[1, c])
        total = part(own2, span)[...] + jnp.sum(part(recv2, span)[...].astype(F32), axis=0)
        projected = total.astype(BF16).astype(F32)
        hidden = (part(res_v, span)[...].astype(F32) + projected).astype(BF16).astype(F32)
        part(hidden_v, span)[...] = hidden
        part(rows_own, span)[0] = (hidden * part(gain_v, span)[...][None]).astype(BF16)
        to_chips(2, c, part(rows_own, span))
        squares.append(jnp.sum(hidden * hidden, axis=1, keepdims=True))
        if c == chunks - 1:
            send_meta()

    def routing_table():
        for copy in smalls[1:]:
            copy.wait()
        lane = lax.broadcasted_iota(jnp.int32, (rows, META), 1).astype(F32)
        square = (rows, rows)
        diagonal = lax.broadcasted_iota(jnp.int32, square, 0) == lax.broadcasted_iota(jnp.int32, square, 1)
        ids = ids_v[...].astype(F32)
        weights = gw_v[...].astype(F32)
        block = jnp.zeros((rows, META), F32)
        for k in range(ids.shape[0]):
            expert = jnp.sum(jnp.where(diagonal, ids[k : k + 1], 0.0), axis=1, keepdims=True)
            weight = jnp.sum(jnp.where(diagonal, weights[k : k + 1], 0.0), axis=1, keepdims=True)
            block = block + jnp.where(lane == expert, weight, 0.0)
        table_v[...] = block

    def send_meta():
        mean = sum(squares[1:], squares[0]) / features
        scale = lax.rsqrt(mean + 1e-06)
        lane = lax.broadcasted_iota(jnp.int32, (rows, META), 1)
        meta_own[0] = jnp.where(lane == experts_all, scale, table_v[...])
        to_chips(2, chunks, meta_own)

    def forward(c, span):
        wait_bytes(peers(part(rows_own, span)), stage_recv.at[2, c])
        to_sibling(3, c, part(rows_own, span), part(rows_sib, span))
        if c == chunks - 1:
            wait_bytes(peers(meta_own), stage_recv.at[2, chunks])
            to_sibling(3, chunks, meta_own, meta_sib)

    def experts(c, span):
        need(wg_copies[c])
        need(wu_copies[c])
        wait_bytes(part(rows_sib, span), stage_recv.at[3, c])
        both = jnp.concatenate(
            [part(ref, span)[...].astype(F32).reshape(half, span[1]) for ref in (rows_own, rows_sib)], axis=0
        ).astype(BF16)
        for member in range(members):
            gate = jnp.dot(both, part(wg_v, span, 1)[member], preferred_element_type=F32)
            up = jnp.dot(both, part(wu_v, span, 1)[member], preferred_element_type=F32)
            acc_gate[member] = gate if c == 0 else acc_gate[member] + gate
            acc_up[member] = up if c == 0 else acc_up[member] + up

    def activate():
        wait_bytes(meta_sib, stage_recv.at[3, chunks])
        block = jnp.concatenate([meta_own[...].reshape(half, META), meta_sib[...].reshape(half, META)], axis=0)
        lane = lax.broadcasted_iota(jnp.int32, block.shape, 1)
        scale = block[:, experts_all : experts_all + 1]
        for member in range(members):
            weight = jnp.sum(
                jnp.where(lane == group * members + member, block, 0.0), axis=1, keepdims=True
            )
            gate = acc_gate[member] * scale
            up = acc_up[member] * scale
            act_v[member] = (gate / (1.0 + jnp.exp(-gate)) * up * weight).astype(BF16)

    def down(c, span):
        need(wd_copies[c])
        product = jnp.dot(act_v[0], part(wd_v, span)[0], preferred_element_type=F32)
        for member in range(1, members):
            product = product + jnp.dot(act_v[member], part(wd_v, span)[member], preferred_element_type=F32)
        split(product, part(keep4, span), part(send4, span))
        to_sibling(4, c, part(send4, span), part(recv4, span))

    def add_sibling_down(c, span):
        wait_bytes(part(recv4, span), stage_recv.at[4, c])
        total = part(keep4, span)[...] + part(recv4, span)[...].astype(F32)
        part(own5, span)[...] = total[0]
        part(send5, span)[...] = total[1:].astype(BF16)
        to_owners(5, c, part(send5, span), part(recv5, span))

    def write_out(c, span):
        return pltpu.make_async_copy(part(out_v, span), part(out_hbm, span), out_sem.at[c])

    def finish(c, span):
        wait_bytes(part(recv5, span), stage_recv.at[5, c])
        total = part(own5, span)[...] + jnp.sum(part(recv5, span)[...].astype(F32), axis=0)
        part(out_v, span)[...] = (part(hidden_v, span)[...] + total).astype(BF16)
        write_out(c, span).start()

    def fetches_after(stage, c):
        if stage is project:
            return 1 if c < chunks - 3 else 0
        if stage is add_sibling:
            return 2 if c == chunks - 1 else 0
        return 1

    def pipeline(stages, pieces):
        unit = features / 7
        steps = [
            ((span[0] + span[1]) / unit + LAGS[s], s, c, stage)
            for s, stage in enumerate(stages)
            for c, span in enumerate(pieces)
        ]
        for _, _, c, stage in sorted(steps, key=lambda step: step[:3]):
            stage(c, pieces[c])
            fetch_more(fetches_after(stage, c))

    pipeline([project, add_sibling, finish_hidden, forward, experts], spans)
    activate()
    pipeline([down, add_sibling_down, finish], down_spans)

    for c, span in enumerate(spans):
        wait_bytes(part(send1, span), stage_send.at[0, c])
        wait_bytes(part(send2, span), stage_send.at[1, c])
        wait_bytes(peers(part(rows_own, span)), stage_send.at[2, c])
        wait_bytes(part(rows_own, span), stage_send.at[3, c])
    for c, span in enumerate(down_spans):
        wait_bytes(part(send4, span), stage_send.at[4, c])
        wait_bytes(part(send5, span), stage_send.at[5, c])
        write_out(c, span).wait()
    wait_bytes(peers(meta_own), stage_send.at[2, chunks])
    wait_bytes(meta_own, stage_send.at[3, chunks])


def on_device(
    attn_heads, out_proj, residual_in, norm_gain, expert_ids, gate_weights, w_gate, w_up, w_down
):
    rows, features = residual_in.shape
    tokens, heads = attn_heads.shape
    groups = lax.axis_size("group")
    tensors = lax.axis_size("tensor")
    members, _, units = w_gate.shape
    chips = groups // 2 * tensors
    experts_all = groups * members
    spans = column_chunks(features, UNITS, True)
    down_spans = column_chunks(features, UNITS, False)
    chunks = max(len(spans), len(down_spans))
    dims = (spans, down_spans, chips, tensors, rows, members, experts_all)

    def vmem(shape, dtype):
        return pltpu.VMEM(shape, dtype)

    exchange = [
        vmem((chips, rows, features), F32),
        vmem((chips, rows, features), BF16),
        vmem((chips, rows, features), BF16),
        vmem((rows, features), F32),
        vmem((chips - 1, rows, features), BF16),
        vmem((chips - 1, rows, features), BF16),
    ]
    scratch = [
        vmem((tokens, heads), BF16),
        vmem((tokens // rows, rows, heads), F32),
        vmem((tokens, heads), BF16),
        vmem((rows, features), BF16),
        vmem((features,), F32),
        vmem(expert_ids.shape[::-1], expert_ids.dtype),
        vmem(gate_weights.shape[::-1], gate_weights.dtype),
        vmem((heads, features), BF16),
        vmem((members, features, units), BF16),
        vmem((members, features, units), BF16),
        vmem((members, units, features), BF16),
        *exchange,
        vmem((rows, features), F32),
        vmem((rows, META), F32),
        vmem((chips, rows, features), BF16),
        vmem((chips, rows, features), BF16),
        vmem((chips, rows, META), F32),
        vmem((chips, rows, META), F32),
        vmem((members, tokens, units), F32),
        vmem((members, tokens, units), F32),
        vmem((members, tokens, units), BF16),
        *exchange,
        vmem((rows, features), BF16),
        pltpu.SemaphoreType.DMA((5,)),
        pltpu.SemaphoreType.DMA((chunks,)),
        pltpu.SemaphoreType.DMA((chunks,)),
        pltpu.SemaphoreType.DMA((chunks,)),
        pltpu.SemaphoreType.DMA((chunks,)),
        pltpu.SemaphoreType.DMA((chunks,)),
        pltpu.SemaphoreType.DMA((6, chunks + 1)),
        pltpu.SemaphoreType.DMA((6, chunks + 1)),
    ]
    weights = out_proj.size + w_gate.size + w_up.size + w_down.size
    return pl.pallas_call(
        functools.partial(kernel, dims),
        out_shape=jax.ShapeDtypeStruct((rows, features), BF16),
        in_specs=[pl.BlockSpec(memory_space=pl.ANY)] * 9,
        out_specs=pl.BlockSpec(memory_space=pl.ANY),
        scratch_shapes=scratch,
        cost_estimate=pl.CostEstimate(
            flops=2 * tokens * weights, bytes_accessed=2 * weights, transcendentals=0
        ),
        compiler_params=pltpu.CompilerParams(
            collective_id=0, has_side_effects=True, vmem_limit_bytes=56 * 1024 * 1024
        ),
        name="projected_experts",
    )(
        attn_heads, out_proj, residual_in, norm_gain,
        expert_ids.T, gate_weights.T, w_gate, w_up, w_down,
    )


def solution(mesh):
    placed = (
        P("dp", ("group", "tensor")),
        P(("group", "tensor"), None),
        P(("dp", "group", "tensor"), None),
        P(),
        P(("dp", "group", "tensor"), None),
        P(("dp", "group", "tensor"), None),
        P("group", None, "tensor"),
        P("group", None, "tensor"),
        P("group", "tensor", None),
    )
    return jax.shard_map(
        on_device,
        mesh=mesh,
        in_specs=placed,
        out_specs=P(("dp", "group", "tensor"), None),
        check_vma=False,
    )
```

```python
import functools

import jax
import jax.numpy as jnp
from jax import lax
from jax.experimental import pallas as pl
from jax.experimental.pallas import tpu as pltpu
from jax.sharding import PartitionSpec as P

MESH = pl.DeviceIdType.MESH
F32 = jnp.float32
BF16 = jnp.bfloat16
UNITS = 2
META = 128
LAGS = (0, 3, 9, 15, 18)


def column_chunks(features, units, first_short):
    tile = 256 if features % 256 == 0 else 128
    count = features // tile
    sizes = [units] * (count // units) + ([count % units] if count % units else [])
    if first_short:
        sizes = sizes[::-1]
    starts = [sum(sizes[:i]) for i in range(len(sizes))]
    return tuple((start * tile, size * tile) for start, size in zip(starts, sizes))


def kernel(
    dims,
    attn_hbm, wo_hbm, res_hbm, gain_hbm, ids_hbm, gw_hbm, wg_hbm, wu_hbm, wd_hbm,
    out_hbm,
    attn_v, attn_blocks, attn_p, res_v, gain_v, ids_v, gw_v,
    wo_v, wg_v, wu_v, wd_v,
    keep1, send1, recv1, own2, send2, recv2, hidden_v, table_v,
    rows_own, rows_sib, meta_own, meta_sib,
    acc_gate, acc_up, act_v,
    keep4, send4, recv4, own5, send5, recv5, out_v,
    small_sem, wo_sem, wg_sem, wu_sem, wd_sem, out_sem,
    stage_send, stage_recv,
):
    spans, down_spans, chips, tensors, rows, members, experts_all = dims
    chunks, down_chunks = len(spans), len(down_spans)
    features = res_v.shape[1]
    half = chips * rows
    group, tensor = lax.axis_index("group"), lax.axis_index("tensor")
    high, low = lax.div(group, 2), lax.rem(group, 2)
    place = high * tensors + tensor

    def device(position, side):
        position = lax.rem(position + chips, chips)
        return {"group": lax.div(position, tensors) * 2 + side, "tensor": lax.rem(position, tensors)}

    sibling = {"group": high * 2 + 1 - low, "tensor": tensor}

    barrier = pltpu.get_barrier_semaphore()
    pl.semaphore_signal(barrier, inc=1, device_id=sibling, device_id_type=MESH)
    for offset in range(1, chips):
        pl.semaphore_signal(
            barrier, inc=1, device_id=device(place + offset, low), device_id_type=MESH
        )

    def part(ref, span, axis=-1):
        index = [slice(None)] * len(ref.shape)
        index[axis] = pl.ds(*span)
        return ref.at[tuple(index)]

    smalls = [
        pltpu.make_async_copy(src, dst, small_sem.at[i])
        for i, (src, dst) in enumerate(
            [(attn_hbm, attn_v), (res_hbm, res_v), (gain_hbm, gain_v), (ids_hbm, ids_v), (gw_hbm, gw_v)]
        )
    ]
    def fetches(src, dst, sems, pieces, axis):
        return [
            pltpu.make_async_copy(part(src, span, axis), part(dst, span, axis), sems.at[c])
            for c, span in enumerate(pieces)
        ]

    wo_copies = fetches(wo_hbm, wo_v, wo_sem, spans, 1)
    wg_copies = fetches(wg_hbm, wg_v, wg_sem, spans, 1)
    wu_copies = fetches(wu_hbm, wu_v, wu_sem, spans, 1)
    wd_copies = fetches(wd_hbm, wd_v, wd_sem, down_spans, 2)
    queue = list(wo_copies)
    for gate_copy, up_copy in zip(wg_copies, wu_copies):
        queue += [gate_copy, up_copy]
    queue += wd_copies

    def fetch_more(count):
        for _ in range(min(count, len(queue))):
            queue.pop(0).start()

    def need(copy):
        while any(copy is later for later in queue):
            fetch_more(1)
        copy.wait()

    smalls[0].start()
    fetch_more(1)
    for copy in smalls[1:]:
        copy.start()
    fetch_more(2)

    def wait_bytes(ref, sem):
        pltpu.make_async_copy(ref, ref, sem).wait()

    def to_sibling(stage, c, src, dst):
        pltpu.make_async_remote_copy(
            src_ref=src, dst_ref=dst, send_sem=stage_send.at[stage, c],
            recv_sem=stage_recv.at[stage, c], device_id=sibling, device_id_type=MESH,
        ).start()

    def to_owners(stage, c, src, dst):
        for offset in range(1, chips):
            pltpu.make_async_remote_copy(
                src_ref=src.at[offset - 1], dst_ref=dst.at[offset - 1],
                send_sem=stage_send.at[stage, c], recv_sem=stage_recv.at[stage, c],
                device_id=device(place - offset, low), device_id_type=MESH,
            ).start()

    def to_chips(stage, c, block):
        for offset in range(1, chips):
            pltpu.make_async_remote_copy(
                src_ref=block.at[0], dst_ref=block.at[offset],
                send_sem=stage_send.at[stage, c], recv_sem=stage_recv.at[stage, c],
                device_id=device(place + offset, low), device_id_type=MESH,
            ).start()

    def peers(block):
        return block.at[pl.ds(1, chips - 1)]

    smalls[0].wait()
    attn_blocks[...] = attn_v[...].astype(F32).reshape(attn_blocks.shape)
    picked = []
    for side in (low, 1 - low):
        for offset in range(chips):
            position = lax.rem(place - offset + chips, chips)
            owner = (lax.div(position, tensors) * 2 + side) * tensors + lax.rem(position, tensors)
            picked.append(attn_blocks[owner])
    attn_p[...] = jnp.concatenate(picked, axis=0).astype(BF16)

    def split(product, keep, send):
        width = product.shape[1]
        keep[...] = product[:half].reshape(chips, rows, width)
        send[...] = product[half:].reshape(chips, rows, width).astype(BF16)

    def project(c, span):
        need(wo_copies[c])
        product = jnp.dot(attn_p[...], part(wo_v, span)[...], preferred_element_type=F32)
        split(product, part(keep1, span), part(send1, span))
        if c == 0:
            pl.semaphore_wait(barrier, chips)
        to_sibling(0, c, part(send1, span), part(recv1, span))
        if c == chunks - 1:
            routing_table()

    def add_sibling(c, span):
        wait_bytes(part(recv1, span), stage_recv.at[0, c])
        total = part(keep1, span)[...] + part(recv1, span)[...].astype(F32)
        part(own2, span)[...] = total[0]
        part(send2, span)[...] = total[1:].astype(BF16)
        to_owners(1, c, part(send2, span), part(recv2, span))

    squares = []

    def finish_hidden(c, span):
        wait_bytes(part(recv2, span), stage_recv.at[1, c])
        total = part(own2, span)[...] + jnp.sum(part(recv2, span)[...].astype(F32), axis=0)
        projected = total.astype(BF16).astype(F32)
        hidden = (part(res_v, span)[...].astype(F32) + projected).astype(BF16).astype(F32)
        part(hidden_v, span)[...] = hidden
        part(rows_own, span)[0] = (hidden * part(gain_v, span)[...][None]).astype(BF16)
        to_chips(2, c, part(rows_own, span))
        squares.append(jnp.sum(hidden * hidden, axis=1, keepdims=True))
        if c == chunks - 1:
            send_meta()

    def routing_table():
        for copy in smalls[1:]:
            copy.wait()
        lane = lax.broadcasted_iota(jnp.int32, (rows, META), 1).astype(F32)
        square = (rows, rows)
        diagonal = lax.broadcasted_iota(jnp.int32, square, 0) == lax.broadcasted_iota(jnp.int32, square, 1)
        ids = ids_v[...].astype(F32)
        weights = gw_v[...].astype(F32)
        block = jnp.zeros((rows, META), F32)
        for k in range(ids.shape[0]):
            expert = jnp.sum(jnp.where(diagonal, ids[k : k + 1], 0.0), axis=1, keepdims=True)
            weight = jnp.sum(jnp.where(diagonal, weights[k : k + 1], 0.0), axis=1, keepdims=True)
            block = block + jnp.where(lane == expert, weight, 0.0)
        table_v[...] = block

    def send_meta():
        mean = sum(squares[1:], squares[0]) / features
        scale = lax.rsqrt(mean + 1e-06)
        lane = lax.broadcasted_iota(jnp.int32, (rows, META), 1)
        meta_own[0] = jnp.where(lane == experts_all, scale, table_v[...])
        to_chips(2, chunks, meta_own)

    def forward(c, span):
        wait_bytes(peers(part(rows_own, span)), stage_recv.at[2, c])
        to_sibling(3, c, part(rows_own, span), part(rows_sib, span))
        if c == chunks - 1:
            wait_bytes(peers(meta_own), stage_recv.at[2, chunks])
            to_sibling(3, chunks, meta_own, meta_sib)

    def experts(c, span):
        need(wg_copies[c])
        need(wu_copies[c])
        wait_bytes(part(rows_sib, span), stage_recv.at[3, c])
        both = jnp.concatenate(
            [part(ref, span)[...].astype(F32).reshape(half, span[1]) for ref in (rows_own, rows_sib)], axis=0
        ).astype(BF16)
        for member in range(members):
            gate = jnp.dot(both, part(wg_v, span, 1)[member], preferred_element_type=F32)
            up = jnp.dot(both, part(wu_v, span, 1)[member], preferred_element_type=F32)
            acc_gate[member] = gate if c == 0 else acc_gate[member] + gate
            acc_up[member] = up if c == 0 else acc_up[member] + up

    def activate():
        wait_bytes(meta_sib, stage_recv.at[3, chunks])
        block = jnp.concatenate([meta_own[...].reshape(half, META), meta_sib[...].reshape(half, META)], axis=0)
        lane = lax.broadcasted_iota(jnp.int32, block.shape, 1)
        scale = block[:, experts_all : experts_all + 1]
        for member in range(members):
            weight = jnp.sum(
                jnp.where(lane == group * members + member, block, 0.0), axis=1, keepdims=True
            )
            gate = acc_gate[member] * scale
            up = acc_up[member] * scale
            act_v[member] = (gate / (1.0 + jnp.exp(-gate)) * up * weight).astype(BF16)

    def down(c, span):
        need(wd_copies[c])
        product = jnp.dot(act_v[0], part(wd_v, span)[0], preferred_element_type=F32)
        for member in range(1, members):
            product = product + jnp.dot(act_v[member], part(wd_v, span)[member], preferred_element_type=F32)
        split(product, part(keep4, span), part(send4, span))
        to_sibling(4, c, part(send4, span), part(recv4, span))

    def add_sibling_down(c, span):
        wait_bytes(part(recv4, span), stage_recv.at[4, c])
        total = part(keep4, span)[...] + part(recv4, span)[...].astype(F32)
        part(own5, span)[...] = total[0]
        part(send5, span)[...] = total[1:].astype(BF16)
        to_owners(5, c, part(send5, span), part(recv5, span))

    def write_out(c, span):
        return pltpu.make_async_copy(part(out_v, span), part(out_hbm, span), out_sem.at[c])

    def finish(c, span):
        wait_bytes(part(recv5, span), stage_recv.at[5, c])
        total = part(own5, span)[...] + jnp.sum(part(recv5, span)[...].astype(F32), axis=0)
        part(out_v, span)[...] = (part(hidden_v, span)[...] + total).astype(BF16)
        write_out(c, span).start()

    def fetches_after(stage, c):
        if stage is project:
            return 1 if c < chunks - 3 else 0
        if stage is add_sibling:
            return 2 if c == chunks - 1 else 0
        return 1

    def pipeline(stages, pieces):
        unit = features / 7
        steps = [
            ((span[0] + span[1]) / unit + LAGS[s], s, c, stage)
            for s, stage in enumerate(stages)
            for c, span in enumerate(pieces)
        ]
        for _, _, c, stage in sorted(steps, key=lambda step: step[:3]):
            stage(c, pieces[c])
            fetch_more(fetches_after(stage, c))

    pipeline([project, add_sibling, finish_hidden, forward, experts], spans)
    activate()
    pipeline([down, add_sibling_down, finish], down_spans)

    for c, span in enumerate(spans):
        wait_bytes(part(send1, span), stage_send.at[0, c])
        wait_bytes(part(send2, span), stage_send.at[1, c])
        wait_bytes(peers(part(rows_own, span)), stage_send.at[2, c])
        wait_bytes(part(rows_own, span), stage_send.at[3, c])
    for c, span in enumerate(down_spans):
        wait_bytes(part(send4, span), stage_send.at[4, c])
        wait_bytes(part(send5, span), stage_send.at[5, c])
        write_out(c, span).wait()
    wait_bytes(peers(meta_own), stage_send.at[2, chunks])
    wait_bytes(meta_own, stage_send.at[3, chunks])


def on_device(
    attn_heads, out_proj, residual_in, norm_gain, expert_ids, gate_weights, w_gate, w_up, w_down
):
    rows, features = residual_in.shape
    tokens, heads = attn_heads.shape
    groups = lax.axis_size("group")
    tensors = lax.axis_size("tensor")
    members, _, units = w_gate.shape
    chips = groups // 2 * tensors
    experts_all = groups * members
    spans = column_chunks(features, UNITS, True)
    down_spans = column_chunks(features, UNITS, False)
    chunks = max(len(spans), len(down_spans))
    dims = (spans, down_spans, chips, tensors, rows, members, experts_all)

    def vmem(shape, dtype):
        return pltpu.VMEM(shape, dtype)

    exchange = [
        vmem((chips, rows, features), F32),
        vmem((chips, rows, features), BF16),
        vmem((chips, rows, features), BF16),
        vmem((rows, features), F32),
        vmem((chips - 1, rows, features), BF16),
        vmem((chips - 1, rows, features), BF16),
    ]
    scratch = [
        vmem((tokens, heads), BF16),
        vmem((tokens // rows, rows, heads), F32),
        vmem((tokens, heads), BF16),
        vmem((rows, features), BF16),
        vmem((features,), F32),
        vmem(expert_ids.shape[::-1], expert_ids.dtype),
        vmem(gate_weights.shape[::-1], gate_weights.dtype),
        vmem((heads, features), BF16),
        vmem((members, features, units), BF16),
        vmem((members, features, units), BF16),
        vmem((members, units, features), BF16),
        *exchange,
        vmem((rows, features), F32),
        vmem((rows, META), F32),
        vmem((chips, rows, features), BF16),
        vmem((chips, rows, features), BF16),
        vmem((chips, rows, META), F32),
        vmem((chips, rows, META), F32),
        vmem((members, tokens, units), F32),
        vmem((members, tokens, units), F32),
        vmem((members, tokens, units), BF16),
        *exchange,
        vmem((rows, features), BF16),
        pltpu.SemaphoreType.DMA((5,)),
        pltpu.SemaphoreType.DMA((chunks,)),
        pltpu.SemaphoreType.DMA((chunks,)),
        pltpu.SemaphoreType.DMA((chunks,)),
        pltpu.SemaphoreType.DMA((chunks,)),
        pltpu.SemaphoreType.DMA((chunks,)),
        pltpu.SemaphoreType.DMA((6, chunks + 1)),
        pltpu.SemaphoreType.DMA((6, chunks + 1)),
    ]
    weights = out_proj.size + w_gate.size + w_up.size + w_down.size
    return pl.pallas_call(
        functools.partial(kernel, dims),
        out_shape=jax.ShapeDtypeStruct((rows, features), BF16),
        in_specs=[pl.BlockSpec(memory_space=pl.ANY)] * 9,
        out_specs=pl.BlockSpec(memory_space=pl.ANY),
        scratch_shapes=scratch,
        cost_estimate=pl.CostEstimate(
            flops=2 * tokens * weights, bytes_accessed=2 * weights, transcendentals=0
        ),
        compiler_params=pltpu.CompilerParams(
            collective_id=0, has_side_effects=True, vmem_limit_bytes=56 * 1024 * 1024
        ),
        name="projected_experts",
    )(
        attn_heads, out_proj, residual_in, norm_gain,
        expert_ids.T, gate_weights.T, w_gate, w_up, w_down,
    )


def solution(mesh):
    placed = (
        P("dp", ("group", "tensor")),
        P(("group", "tensor"), None),
        P(("dp", "group", "tensor"), None),
        P(),
        P(("dp", "group", "tensor"), None),
        P(("dp", "group", "tensor"), None),
        P("group", None, "tensor"),
        P("group", None, "tensor"),
        P("group", "tensor", None),
    )
    return jax.shard_map(
        on_device,
        mesh=mesh,
        in_specs=placed,
        out_specs=P(("dp", "group", "tensor"), None),
        check_vma=False,
    )
```

```python
import functools

import jax
import jax.numpy as jnp
from jax import lax
from jax.experimental import pallas as pl
from jax.experimental.pallas import tpu as pltpu
from jax.sharding import PartitionSpec as P

MESH = pl.DeviceIdType.MESH
F32 = jnp.float32
BF16 = jnp.bfloat16
UNITS = 2
META = 128
LAGS = (0, 2, 8, 14, 16)


def column_chunks(features, units, first_short):
    tile = 256 if features % 256 == 0 else 128
    count = features // tile
    sizes = [units] * (count // units) + ([count % units] if count % units else [])
    if first_short:
        sizes = sizes[::-1]
    starts = [sum(sizes[:i]) for i in range(len(sizes))]
    return tuple((start * tile, size * tile) for start, size in zip(starts, sizes))


def kernel(
    dims,
    attn_hbm, wo_hbm, res_hbm, gain_hbm, ids_hbm, gw_hbm, wg_hbm, wu_hbm, wd_hbm,
    base_hbm, landed_hbm,
    attn_v, attn_blocks, attn_p, res_v, gain_v, ids_v, gw_v,
    wo_v, wg_v, wu_v, wd_v,
    keep1, send1, recv1, own2, send2, recv2, hidden_v, table_v,
    rows_own, rows_sib, meta_own, meta_sib,
    acc_gate, acc_up, act_v,
    keep4, send4, recv4, own5, send5,
    small_sem, wo_sem, wg_sem, wu_sem, wd_sem, out_sem,
    stage_send, stage_recv,
):
    spans, down_spans, chips, tensors, rows, members, experts_all = dims
    chunks, down_chunks = len(spans), len(down_spans)
    features = res_v.shape[1]
    half = chips * rows
    group, tensor = lax.axis_index("group"), lax.axis_index("tensor")
    high, low = lax.div(group, 2), lax.rem(group, 2)
    place = high * tensors + tensor

    def device(position, side):
        position = lax.rem(position + chips, chips)
        return {"group": lax.div(position, tensors) * 2 + side, "tensor": lax.rem(position, tensors)}

    sibling = {"group": high * 2 + 1 - low, "tensor": tensor}

    barrier = pltpu.get_barrier_semaphore()
    pl.semaphore_signal(barrier, inc=1, device_id=sibling, device_id_type=MESH)
    for offset in range(1, chips):
        pl.semaphore_signal(
            barrier, inc=1, device_id=device(place + offset, low), device_id_type=MESH
        )

    def part(ref, span, axis=-1):
        index = [slice(None)] * len(ref.shape)
        index[axis] = pl.ds(*span)
        return ref.at[tuple(index)]

    smalls = [
        pltpu.make_async_copy(src, dst, small_sem.at[i])
        for i, (src, dst) in enumerate(
            [(attn_hbm, attn_v), (res_hbm, res_v), (gain_hbm, gain_v), (ids_hbm, ids_v), (gw_hbm, gw_v)]
        )
    ]
    def fetches(src, dst, sems, pieces, axis):
        return [
            pltpu.make_async_copy(part(src, span, axis), part(dst, span, axis), sems.at[c])
            for c, span in enumerate(pieces)
        ]

    wo_copies = fetches(wo_hbm, wo_v, wo_sem, spans, 1)
    wg_copies = fetches(wg_hbm, wg_v, wg_sem, spans, 1)
    wu_copies = fetches(wu_hbm, wu_v, wu_sem, spans, 1)
    wd_copies = fetches(wd_hbm, wd_v, wd_sem, down_spans, 2)
    queue = list(wo_copies)
    for gate_copy, up_copy in zip(wg_copies, wu_copies):
        queue += [gate_copy, up_copy]
    queue += wd_copies

    def fetch_more(count):
        for _ in range(min(count, len(queue))):
            queue.pop(0).start()

    def need(copy):
        while any(copy is later for later in queue):
            fetch_more(1)
        copy.wait()

    smalls[0].start()
    fetch_more(1)
    for copy in smalls[1:]:
        copy.start()
    fetch_more(2)

    def wait_bytes(ref, sem):
        pltpu.make_async_copy(ref, ref, sem).wait()

    def to_sibling(stage, c, src, dst):
        pltpu.make_async_remote_copy(
            src_ref=src, dst_ref=dst, send_sem=stage_send.at[stage, c],
            recv_sem=stage_recv.at[stage, c], device_id=sibling, device_id_type=MESH,
        ).start()

    def to_owners(stage, c, src, dst):
        for offset in range(1, chips):
            pltpu.make_async_remote_copy(
                src_ref=src.at[offset - 1], dst_ref=dst.at[offset - 1],
                send_sem=stage_send.at[stage, c], recv_sem=stage_recv.at[stage, c],
                device_id=device(place - offset, low), device_id_type=MESH,
            ).start()

    def to_chips(stage, c, block):
        for offset in range(1, chips):
            pltpu.make_async_remote_copy(
                src_ref=block.at[0], dst_ref=block.at[offset],
                send_sem=stage_send.at[stage, c], recv_sem=stage_recv.at[stage, c],
                device_id=device(place + offset, low), device_id_type=MESH,
            ).start()

    def peers(block):
        return block.at[pl.ds(1, chips - 1)]

    smalls[0].wait()
    attn_blocks[...] = attn_v[...].astype(F32).reshape(attn_blocks.shape)
    picked = []
    for side in (low, 1 - low):
        for offset in range(chips):
            position = lax.rem(place - offset + chips, chips)
            owner = (lax.div(position, tensors) * 2 + side) * tensors + lax.rem(position, tensors)
            picked.append(attn_blocks[owner])
    attn_p[...] = jnp.concatenate(picked, axis=0).astype(BF16)

    def split(product, keep, send):
        width = product.shape[1]
        keep[...] = product[:half].reshape(chips, rows, width)
        send[...] = product[half:].reshape(chips, rows, width).astype(BF16)

    def project(c, span):
        need(wo_copies[c])
        product = jnp.dot(attn_p[...], part(wo_v, span)[...], preferred_element_type=F32)
        split(product, part(keep1, span), part(send1, span))
        if c == 0:
            pl.semaphore_wait(barrier, chips)
        to_sibling(0, c, part(send1, span), part(recv1, span))
        if c == chunks - 1:
            routing_table()

    def add_sibling(c, span):
        wait_bytes(part(recv1, span), stage_recv.at[0, c])
        total = part(keep1, span)[...] + part(recv1, span)[...].astype(F32)
        part(own2, span)[...] = total[0]
        part(send2, span)[...] = total[1:].astype(BF16)
        to_owners(1, c, part(send2, span), part(recv2, span))

    squares = []

    def finish_hidden(c, span):
        wait_bytes(part(recv2, span), stage_recv.at[1, c])
        total = part(own2, span)[...] + jnp.sum(part(recv2, span)[...].astype(F32), axis=0)
        projected = total.astype(BF16).astype(F32)
        hidden = (part(res_v, span)[...].astype(F32) + projected).astype(BF16).astype(F32)
        part(hidden_v, span)[...] = hidden
        part(rows_own, span)[0] = (hidden * part(gain_v, span)[...][None]).astype(BF16)
        to_chips(2, c, part(rows_own, span))
        squares.append(jnp.sum(hidden * hidden, axis=1, keepdims=True))
        if c == chunks - 1:
            send_meta()

    def routing_table():
        for copy in smalls[1:]:
            copy.wait()
        lane = lax.broadcasted_iota(jnp.int32, (rows, META), 1).astype(F32)
        square = (rows, rows)
        diagonal = lax.broadcasted_iota(jnp.int32, square, 0) == lax.broadcasted_iota(jnp.int32, square, 1)
        ids = ids_v[...].astype(F32)
        weights = gw_v[...].astype(F32)
        block = jnp.zeros((rows, META), F32)
        for k in range(ids.shape[0]):
            expert = jnp.sum(jnp.where(diagonal, ids[k : k + 1], 0.0), axis=1, keepdims=True)
            weight = jnp.sum(jnp.where(diagonal, weights[k : k + 1], 0.0), axis=1, keepdims=True)
            block = block + jnp.where(lane == expert, weight, 0.0)
        table_v[...] = block

    def send_meta():
        mean = sum(squares[1:], squares[0]) / features
        scale = lax.rsqrt(mean + 1e-06)
        lane = lax.broadcasted_iota(jnp.int32, (rows, META), 1)
        meta_own[0] = jnp.where(lane == experts_all, scale, table_v[...])
        to_chips(2, chunks, meta_own)

    def forward(c, span):
        wait_bytes(peers(part(rows_own, span)), stage_recv.at[2, c])
        to_sibling(3, c, part(rows_own, span), part(rows_sib, span))
        if c == chunks - 1:
            wait_bytes(peers(meta_own), stage_recv.at[2, chunks])
            to_sibling(3, chunks, meta_own, meta_sib)

    def experts(c, span):
        need(wg_copies[c])
        need(wu_copies[c])
        wait_bytes(part(rows_sib, span), stage_recv.at[3, c])
        both = jnp.concatenate(
            [part(ref, span)[...].astype(F32).reshape(half, span[1]) for ref in (rows_own, rows_sib)], axis=0
        ).astype(BF16)
        for member in range(members):
            gate = jnp.dot(both, part(wg_v, span, 1)[member], preferred_element_type=F32)
            up = jnp.dot(both, part(wu_v, span, 1)[member], preferred_element_type=F32)
            acc_gate[member] = gate if c == 0 else acc_gate[member] + gate
            acc_up[member] = up if c == 0 else acc_up[member] + up

    def activate():
        wait_bytes(meta_sib, stage_recv.at[3, chunks])
        block = jnp.concatenate([meta_own[...].reshape(half, META), meta_sib[...].reshape(half, META)], axis=0)
        lane = lax.broadcasted_iota(jnp.int32, block.shape, 1)
        scale = block[:, experts_all : experts_all + 1]
        for member in range(members):
            weight = jnp.sum(
                jnp.where(lane == group * members + member, block, 0.0), axis=1, keepdims=True
            )
            gate = acc_gate[member] * scale
            up = acc_up[member] * scale
            act_v[member] = (gate / (1.0 + jnp.exp(-gate)) * up * weight).astype(BF16)

    def down(c, span):
        need(wd_copies[c])
        product = jnp.dot(act_v[0], part(wd_v, span)[0], preferred_element_type=F32)
        for member in range(1, members):
            product = product + jnp.dot(act_v[member], part(wd_v, span)[member], preferred_element_type=F32)
        split(product, part(keep4, span), part(send4, span))
        to_sibling(4, c, part(send4, span), part(recv4, span))

    def add_sibling_down(c, span):
        wait_bytes(part(recv4, span), stage_recv.at[4, c])
        total = part(keep4, span)[...] + part(recv4, span)[...].astype(F32)
        part(own5, span)[...] = part(hidden_v, span)[...] + total[0]
        part(send5, span)[...] = total[1:].astype(BF16)
        write_base(c, span).start()
        to_owners(5, c, part(send5, span), part(landed_hbm, span))

    def write_base(c, span):
        return pltpu.make_async_copy(part(own5, span), part(base_hbm, span), out_sem.at[c])

    def fetches_after(stage, c):
        if stage is project:
            return 1 if c < chunks - 3 else 0
        if stage is add_sibling:
            return 2 if c == chunks - 1 else 0
        return 1

    def pipeline(stages, pieces):
        unit = features / 7
        steps = [
            ((span[0] + span[1]) / unit + LAGS[s], s, c, stage)
            for s, stage in enumerate(stages)
            for c, span in enumerate(pieces)
        ]
        for _, _, c, stage in sorted(steps, key=lambda step: step[:3]):
            stage(c, pieces[c])
            fetch_more(fetches_after(stage, c))

    pipeline([project, add_sibling, finish_hidden, forward, experts], spans)
    activate()
    pipeline([down, add_sibling_down], down_spans)

    for c, span in enumerate(spans):
        wait_bytes(part(send1, span), stage_send.at[0, c])
        wait_bytes(part(send2, span), stage_send.at[1, c])
        wait_bytes(peers(part(rows_own, span)), stage_send.at[2, c])
        wait_bytes(part(rows_own, span), stage_send.at[3, c])
    for c, span in enumerate(down_spans):
        wait_bytes(part(send4, span), stage_send.at[4, c])
        wait_bytes(part(send5, span), stage_send.at[5, c])
        write_base(c, span).wait()
        wait_bytes(part(landed_hbm, span), stage_recv.at[5, c])
    wait_bytes(peers(meta_own), stage_send.at[2, chunks])
    wait_bytes(meta_own, stage_send.at[3, chunks])


def on_device(
    attn_heads, out_proj, residual_in, norm_gain, expert_ids, gate_weights, w_gate, w_up, w_down
):
    rows, features = residual_in.shape
    tokens, heads = attn_heads.shape
    groups = lax.axis_size("group")
    tensors = lax.axis_size("tensor")
    members, _, units = w_gate.shape
    chips = groups // 2 * tensors
    experts_all = groups * members
    spans = column_chunks(features, UNITS, True)
    down_spans = column_chunks(features, UNITS, False)
    chunks = max(len(spans), len(down_spans))
    dims = (spans, down_spans, chips, tensors, rows, members, experts_all)

    def vmem(shape, dtype):
        return pltpu.VMEM(shape, dtype)

    exchange = [
        vmem((chips, rows, features), F32),
        vmem((chips, rows, features), BF16),
        vmem((chips, rows, features), BF16),
        vmem((rows, features), F32),
        vmem((chips - 1, rows, features), BF16),
        vmem((chips - 1, rows, features), BF16),
    ]
    scratch = [
        vmem((tokens, heads), BF16),
        vmem((tokens // rows, rows, heads), F32),
        vmem((tokens, heads), BF16),
        vmem((rows, features), BF16),
        vmem((features,), F32),
        vmem(expert_ids.shape[::-1], expert_ids.dtype),
        vmem(gate_weights.shape[::-1], gate_weights.dtype),
        vmem((heads, features), BF16),
        vmem((members, features, units), BF16),
        vmem((members, features, units), BF16),
        vmem((members, units, features), BF16),
        *exchange,
        vmem((rows, features), F32),
        vmem((rows, META), F32),
        vmem((chips, rows, features), BF16),
        vmem((chips, rows, features), BF16),
        vmem((chips, rows, META), F32),
        vmem((chips, rows, META), F32),
        vmem((members, tokens, units), F32),
        vmem((members, tokens, units), F32),
        vmem((members, tokens, units), BF16),
        *exchange[:-1],
        pltpu.SemaphoreType.DMA((5,)),
        pltpu.SemaphoreType.DMA((chunks,)),
        pltpu.SemaphoreType.DMA((chunks,)),
        pltpu.SemaphoreType.DMA((chunks,)),
        pltpu.SemaphoreType.DMA((chunks,)),
        pltpu.SemaphoreType.DMA((chunks,)),
        pltpu.SemaphoreType.DMA((6, chunks + 1)),
        pltpu.SemaphoreType.DMA((6, chunks + 1)),
    ]
    weights = out_proj.size + w_gate.size + w_up.size + w_down.size
    base, landed = pl.pallas_call(
        functools.partial(kernel, dims),
        out_shape=(
            jax.ShapeDtypeStruct((rows, features), F32),
            jax.ShapeDtypeStruct((chips - 1, rows, features), BF16),
        ),
        in_specs=[pl.BlockSpec(memory_space=pl.ANY)] * 9,
        out_specs=[pl.BlockSpec(memory_space=pl.ANY)] * 2,
        scratch_shapes=scratch,
        cost_estimate=pl.CostEstimate(
            flops=2 * tokens * weights, bytes_accessed=2 * weights, transcendentals=0
        ),
        compiler_params=pltpu.CompilerParams(
            collective_id=0, has_side_effects=True, vmem_limit_bytes=56 * 1024 * 1024
        ),
        name="projected_experts",
    )(
        attn_heads, out_proj, residual_in, norm_gain,
        expert_ids.T, gate_weights.T, w_gate, w_up, w_down,
    )
    total = base
    for i in range(chips - 1):
        total = total + landed[i].astype(F32)
    return total.astype(BF16)


def solution(mesh):
    placed = (
        P("dp", ("group", "tensor")),
        P(("group", "tensor"), None),
        P(("dp", "group", "tensor"), None),
        P(),
        P(("dp", "group", "tensor"), None),
        P(("dp", "group", "tensor"), None),
        P("group", None, "tensor"),
        P("group", None, "tensor"),
        P("group", "tensor", None),
    )
    return jax.shard_map(
        on_device,
        mesh=mesh,
        in_specs=placed,
        out_specs=P(("dp", "group", "tensor"), None),
        check_vma=False,
    )
```
